256 devices in a mesh: pipe: 8 (over y, x_hi), expert: 32 (over x_lo, z, core).
Axes of the slice: x: 4 (x_hi: 2, x_lo: 2; x = x_hi * 2 + x_lo), y: 4, z: 8, core: 2. Of those that a mesh axis runs over, the one named last changes fastest.
Arguments:
- tokens: bfloat16 [8192, 14336], P('expert', 'pipe'), may hold values from -6 to 6
- cotangent: bfloat16 [8192, 14336], P('expert', 'pipe'), may hold values from -6 to 6
- route_a: int32 [8192, 8], P('expert'), may hold values from 0 to 255, all different within a row; in each aligned block of 256 rows (0 to 255, 256 to 511, ...) at most 16 rows name the same one
- route_b: int32 [8192, 8], P('expert'), may hold values from 0 to 255, all different within a row; in each aligned block of 256 rows (0 to 255, 256 to 511, ...) at most 16 rows name the same one
- gates_a: bfloat16 [8192, 8], P('expert'), may hold values from 0.099609375 to 1
- gates_b: bfloat16 [8192, 8], P('expert'), may hold values from 0.099609375 to 1
- w_up: bfloat16 [32, 14336, 1024], P('expert', 'pipe'), as said below
- w_down: bfloat16 [32, 1024, 14336], P('expert', None, 'pipe'), as said below
Outputs:
- out_y: bfloat16 [8192, 14336], P('expert', 'pipe')
- grad_x: bfloat16 [8192, 14336], P('expert', 'pipe')
- grad_down: bfloat16 [32, 512, 14336], P('expert', None, 'pipe')
The draws below stay inside these ranges and needn't reach their ends.
Inputs may be any that keep to these rules, and one draw needn't show every extreme that they name: `route_a`: each row names 8 different experts. Among the rows of one device no expert is named more than 16 times, and in some device's rows some expert is named exactly 16 times. `route_b`: each row names 8 different experts. Among the rows of one device no expert is named more than 16 times, and in some device's rows some expert is named exactly 16 times. `w_up`: row block k of 1792 rows equals row block 7 - k. `w_down`: column block k of 1792 columns equals column block 7 - k.
All inputs are finite; a program needn't handle non-finite values.
Results may differ from the reference program's by a relative error of at most 0.0065.
Values may be sent and summed in bfloat16 or wider, within the bound.
No kernel may reach another device: no remote copies, remote signals or barrier semaphores. Data moves between devices by JAX's collectives and lax.ppermute only.
A program may use at most 128 MiB of HBM per device.

```python
import math
from functools import partial
import jax
import jax.numpy as jnp
import numpy as np
from jax import lax

D = 7168
EXPERTS = 256
TOP = 8
HID = 1024
TOK_DEV = 256
CAP = 16
SECTIONS = 4
DB = 1792
TOKENS = 8192
N_PIPE = 8
N_EXPERT = 32


def draw_w_up(key, part):
    key = jax.random.fold_in(key, 11)
    base = jax.random.normal(key, (N_EXPERT, D, HID), jnp.float32) * D ** (-0.5)
    mirrored = base.reshape(N_EXPERT, SECTIONS, DB, HID)[:, ::-1].reshape(N_EXPERT, D, HID)
    return jnp.concatenate([base, mirrored], axis=1).astype(jnp.bfloat16)


def draw_w_down(key, part):
    key = jax.random.fold_in(key, 23)
    base = jax.random.normal(key, (N_EXPERT, HID, D), jnp.float32) * HID ** (-0.5)
    mirrored = base.reshape(N_EXPERT, HID, SECTIONS, DB)[:, :, ::-1].reshape(N_EXPERT, HID, D)
    return jnp.concatenate([base, mirrored], axis=2).astype(jnp.bfloat16)


def levels(key, shape, cuts, least, top_value):
    factor_of, own = 1.0, jax.random.fold_in(key, 6)
    for dim, blocks in cuts:
        draws = jnp.exp(jax.random.uniform(jax.random.fold_in(own, dim), (blocks,), jnp.float32, least / len(cuts), top_value / len(cuts)))
        factor_of = factor_of * jnp.repeat(draws, shape[dim] // blocks).reshape([-1 if axis == dim else 1 for axis in range(len(shape))])
    return factor_of


def deal_out(stream_key, own, number, rows, amount, top, limit, slope):
    ranking = jax.random.permutation(stream_key, amount)
    crowded, usual = load_shares(amount, rows * top, limit, slope, True), load_shares(amount, rows * top, limit, slope, False)
    places = jnp.arange(amount)

    def named(lengths, rotation):
        used = int((lengths > 0).sum())
        fixed = max(1, used // 4)
        moved = fixed + (places - fixed + rotation * (used - fixed)) % max(1, amount - fixed)
        return jnp.zeros((amount,), jnp.int32).at[ranking[jnp.where(places < fixed, places, moved)]].set(jnp.asarray(lengths, jnp.int32))

    lengths = jnp.where(number % 4 == 0, named(crowded, number // 4), named(usual, number - number // 4 - 1))
    mixed = jax.random.permutation(jax.random.fold_in(own, 3), amount)
    giver, taker = mixed[0:amount // 2 * 2:2], mixed[1:amount // 2 * 2:2]
    room = jnp.minimum(lengths[giver] - 1, limit - lengths[taker]) // 2
    room = jnp.where((giver == ranking[0]) | (taker == ranking[0]) | (lengths[taker] == 0), 0, jnp.maximum(room, 0))
    moved = jax.random.randint(jax.random.fold_in(own, 4), (amount // 2,), 0, 1 << 20) % (room + 1)
    lengths = lengths.at[giver].add(-moved).at[taker].add(moved)
    members = jnp.searchsorted(jnp.cumsum(lengths), jnp.arange(rows * top), side="right").astype(jnp.int32)
    table = members.reshape(top, rows).T
    table = table[jax.random.permutation(jax.random.fold_in(own, 1), rows)]
    rotation = jax.random.randint(jax.random.fold_in(own, 2), (rows, 1), 0, top)
    return jnp.take_along_axis(table, (jnp.arange(top)[None, :] + rotation) % top, axis=1)


def load_shares(count, total, most, lean, full):
    weights = [(1 << 20) // math.isqrt(rank ** lean) + 1 for rank in range(1, count + 1)]
    largest = most if full else min(most, max(-(-total // count), total * weights[0] // sum(weights)))
    least = 1 if total - largest >= count - 1 else 0
    holding, spare = [largest] + [least] * (count - 1), total - largest - least * (count - 1)
    while spare > 0:
        candidates = [i for i in range(1, count) if holding[i] < largest] or [i for i in range(1, count) if holding[i] < most]
        pool, budget = sum([weights[i] for i in candidates]), spare
        for i in candidates:
            addition = min(most - holding[i], max(1, budget * weights[i] // pool), spare)
            holding[i] = holding[i] + addition
            spare = spare - addition
    return np.array(holding)


def noise(own_key, shape, scale, reach, cuts=(), kind=jnp.bfloat16):
    values = jax.random.normal(own_key, shape, jnp.float32) * scale
    if len(cuts) > 0:
        values = levels(own_key, shape, cuts, -0.22, 0.18) * values
    return jnp.clip(values, min=-reach, max=reach).astype(kind)


def setup_inputs(seed: int = 0) -> dict:
    key_of = jax.random.split(jax.random.key(seed), 9)
    tokens = noise(key_of[0], (TOKENS, N_PIPE * DB), 1.0, 6.0, ((0, 32), (1, 8)))
    cotangent = noise(key_of[1], (TOKENS, N_PIPE * DB), 1.0, 6.0, ((0, 32), (1, 8)))
    route_a_keys = jax.random.split(jax.random.fold_in(key_of[2], 1), TOKENS // TOK_DEV)
    route_a_turns = jax.random.permutation(jax.random.fold_in(key_of[2], 3), TOKENS // TOK_DEV)
    route_a = jax.vmap(lambda own, number: deal_out(jax.random.fold_in(key_of[2], 2), own, number, TOK_DEV, EXPERTS, TOP, CAP, 1))(route_a_keys, route_a_turns).reshape((TOKENS, TOP))
    route_b_keys = jax.random.split(jax.random.fold_in(key_of[3], 1), TOKENS // TOK_DEV)
    route_b_turns = jax.random.permutation(jax.random.fold_in(key_of[3], 3), TOKENS // TOK_DEV)
    route_b = jax.vmap(lambda own, number: deal_out(jax.random.fold_in(key_of[3], 2), own, number, TOK_DEV, EXPERTS, TOP, CAP, 1))(route_b_keys, route_b_turns).reshape((TOKENS, TOP))
    gates_a = jnp.clip(jnp.exp(math.log(1.0) - 2.306499 * jax.random.uniform(key_of[4], (TOKENS, TOP), jnp.float32) ** levels(key_of[4], (TOKENS, TOP), ((0, 32),), -0.2, 0.2)), 0.099609375, 1.0).astype(jnp.bfloat16)
    gates_b = jnp.clip(jnp.exp(math.log(1.0) - 2.306499 * jax.random.uniform(key_of[5], (TOKENS, TOP), jnp.float32) ** levels(key_of[5], (TOKENS, TOP), ((0, 32),), -0.2, 0.2)), 0.099609375, 1.0).astype(jnp.bfloat16)
    w_up = draw_w_up(jax.random.fold_in(key_of[8], 71), 0)
    w_down = draw_w_down(jax.random.fold_in(key_of[8], 71), 0)
    return {"tokens": tokens, "cotangent": cotangent, "route_a": route_a, "route_b": route_b, "gates_a": gates_a, "gates_b": gates_b, "w_up": w_up, "w_down": w_down}


def slot_tables(routing, gate_values, expert_count, capacity):
    flat_routes = routing.reshape(-1).astype(jnp.int32)
    experts_iota = jnp.arange(expert_count, dtype=jnp.int32)
    one_hot = (flat_routes[:, None] == experts_iota[None, :]).astype(jnp.int32)
    running = jnp.cumsum(one_hot, axis=0).astype(jnp.int32) - 1
    position = jnp.sum(running * one_hot, axis=1).astype(jnp.int32)
    slot_ids = jnp.where(flat_routes < expert_count, flat_routes * capacity + position, -1).astype(jnp.int32)
    slot_iota = jnp.arange(expert_count * capacity, dtype=jnp.int32)
    slot_match = slot_ids[None, :] == slot_iota[:, None]
    dispatch_table = jnp.any(slot_match.reshape(expert_count * capacity, routing.shape[0], routing.shape[1]), axis=2).astype(jnp.bfloat16)
    gate_flat = gate_values.reshape(-1).astype(jnp.float32)
    slot_gates = jnp.sum(jnp.where(slot_match, gate_flat[None, :], jnp.zeros((), jnp.float32)), axis=1).astype(jnp.bfloat16)
    return dispatch_table, slot_gates


def flip_columns(array):
    lead = array.shape[:-1]
    return array.reshape(lead + (SECTIONS, DB))[..., ::-1, :].reshape(lead + (SECTIONS * DB,))


def gather_block(operands):
    table, block = operands
    return jnp.dot(table, block, preferred_element_type=jnp.float32).astype(jnp.bfloat16)


def scatter_block(operands):
    table, block = operands
    return jnp.dot(table.T, block, preferred_element_type=jnp.float32).astype(jnp.bfloat16)


def to_expert(array):
    return array.reshape(N_EXPERT, N_EXPERT, CAP, -1).transpose(1, 0, 2, 3).reshape(N_EXPERT, N_EXPERT * CAP, -1)


def from_expert(array):
    return array.reshape(N_EXPERT, N_EXPERT, CAP, -1).transpose(1, 0, 2, 3).reshape(N_EXPERT, N_EXPERT * CAP, -1)


def expert_step(operands):
    rows_x, rows_dy, gate_column, up_weight, down_weight = operands
    gate_float = gate_column.astype(jnp.float32)
    hidden = jnp.dot(rows_x, up_weight, preferred_element_type=jnp.float32)
    sigmoid_h = jax.nn.sigmoid(hidden)
    activated = (hidden * sigmoid_h).astype(jnp.bfloat16)
    expert_out = (gate_float * jnp.dot(activated, down_weight, preferred_element_type=jnp.float32)).astype(jnp.bfloat16)
    d_out = (gate_float * rows_dy.astype(jnp.float32)).astype(jnp.bfloat16)
    d_act = jnp.dot(d_out, down_weight.T, preferred_element_type=jnp.float32)
    d_hidden = (d_act * sigmoid_h * (1.0 + hidden * (1.0 - sigmoid_h))).astype(jnp.bfloat16)
    d_rows = jnp.dot(d_hidden, up_weight.T, preferred_element_type=jnp.float32).astype(jnp.bfloat16)
    weight_grad = jnp.dot(activated.T, d_out, preferred_element_type=jnp.float32).astype(jnp.bfloat16)
    return expert_out, d_rows, weight_grad


def run_batch(inputs, grads_in, routing, gate_values, up_all, down_all):
    tables, slot_gates = jax.vmap(partial(slot_tables, expert_count=N_EXPERT, capacity=CAP))(
        routing.reshape(N_EXPERT, TOK_DEV, TOP), gate_values.reshape(N_EXPERT, TOK_DEV, TOP))
    sent_x = lax.map(gather_block, (tables, inputs.reshape(N_EXPERT, TOK_DEV, D)))
    sent_dy = lax.map(gather_block, (tables, grads_in.reshape(N_EXPERT, TOK_DEV, D)))
    gate_rows = to_expert(slot_gates.reshape(N_EXPERT, N_EXPERT * CAP, 1))
    expert_out, d_rows, weight_grad = lax.map(expert_step, (to_expert(sent_x), to_expert(sent_dy), gate_rows, up_all, down_all))
    layer_out = lax.map(scatter_block, (tables, from_expert(expert_out))).reshape(TOKENS, D)
    grad_tokens = lax.map(scatter_block, (tables, from_expert(d_rows))).reshape(TOKENS, D)
    return layer_out, grad_tokens, weight_grad


def reference(tokens, cotangent, route_a, route_b, gates_a, gates_b, w_up, w_down):
    half_width = SECTIONS * DB
    up_a = w_up[:, :half_width, :]
    up_b = w_up[:, half_width:, :].reshape(N_EXPERT, SECTIONS, DB, HID)[:, ::-1].reshape(N_EXPERT, D, HID)
    down_a = w_down[:, :, :half_width]
    down_b = flip_columns(w_down[:, :, half_width:])
    out_a, grad_a, weight_a = run_batch(tokens[:, :half_width], cotangent[:, :half_width], route_a, gates_a, up_a, down_a)
    out_b, grad_b, weight_b = run_batch(flip_columns(tokens[:, half_width:]), flip_columns(cotangent[:, half_width:]), route_b, gates_b, up_b, down_b)
    weight_a = lax.optimization_barrier(weight_a)
    weight_b = lax.optimization_barrier(weight_b)
    summed = (weight_a.astype(jnp.float32) + weight_b.astype(jnp.float32)).astype(jnp.bfloat16)
    half_rows = HID // 2
    out_y = jnp.concatenate([out_a, flip_columns(out_b)], axis=1)
    grad_x = jnp.concatenate([grad_a, flip_columns(grad_b)], axis=1)
    grad_down = jnp.concatenate([summed[:, :half_rows, :], flip_columns(summed[:, half_rows:, :])], axis=2)
    return out_y, grad_x, grad_down
```

```python
import functools

import jax
import jax.numpy as jnp
from jax import lax
from jax.experimental import pallas as pl
from jax.experimental.pallas import tpu as pltpu
from jax.sharding import PartitionSpec as P

CAP = 16
BF = jnp.bfloat16
F32 = jnp.float32


def params(megabytes):
    return pltpu.CompilerParams(vmem_limit_bytes=megabytes * 1024 * 1024)


def whole(shape):
    return pl.BlockSpec(shape, lambda i, m: (0,) * len(shape))


def dot(a, b, ca, cb):
    return lax.dot_general(a, b, (((ca,), (cb,)), ((), ())), preferred_element_type=F32)


def column_block(width):
    for size in (256, 128):
        if width % size == 0:
            return size
    return width


def dispatch_kernel(side_ref, ra_ref, rb_ref, ga_ref, gb_ref, x_ref, out_ref, plain_ref, gated_ref):
    @pl.when(pl.program_id(0) == 0)
    def _():
        upper = side_ref[1] == 1
        route = jnp.where(upper, rb_ref[...], ra_ref[...])
        gates = jnp.where(upper, gb_ref[...].astype(F32), ga_ref[...].astype(F32))
        top, tokens = route.shape
        slots = plain_ref.shape[0]
        experts = slots // CAP
        expert = lax.broadcasted_iota(jnp.int32, (experts, tokens), 0)
        member = jnp.zeros((experts, tokens), F32)
        gate = jnp.zeros((experts, tokens), F32)
        for k in range(top):
            named = route[k : k + 1, :] == expert
            member = member + jnp.where(named, 1.0, 0.0)
            gate = gate + jnp.where(named, gates[k : k + 1, :], 0.0)
        before = lax.broadcasted_iota(jnp.int32, (tokens, tokens), 0) < lax.broadcasted_iota(
            jnp.int32, (tokens, tokens), 1
        )
        earlier = dot(member.astype(BF), jnp.where(before, 1.0, 0.0).astype(BF), 1, 0)
        place = jnp.where(member > 0.5, earlier, 128.0).astype(BF)
        row = lax.broadcasted_iota(jnp.int32, (slots, experts), 0)
        column = lax.broadcasted_iota(jnp.int32, (slots, experts), 1)
        spread = jnp.where(row // CAP == column, 1.0, 0.0).astype(BF)
        place_rows = dot(spread, place, 1, 0)
        gate_rows = dot(spread, gate.astype(BF), 1, 0)
        slot = lax.broadcasted_iota(jnp.int32, (slots, tokens), 0) % CAP
        hit = place_rows == slot.astype(F32)
        plain_ref[...] = jnp.where(hit, 1.0, 0.0).astype(BF)
        gated_ref[...] = jnp.where(hit, gate_rows, 0.0).astype(BF)

    out_ref[...] = dot(plain_ref[...], x_ref[...], 1, 0).astype(BF)


def dispatch(side, route_a, route_b, gates_a, gates_b, x, slots):
    tokens, width = x.shape
    cols = column_block(width)
    small = whole((route_a.shape[1], tokens))
    return pl.pallas_call(
        dispatch_kernel,
        grid_spec=pltpu.PrefetchScalarGridSpec(
            num_scalar_prefetch=1,
            grid=(width // cols,),
            in_specs=[small] * 4 + [pl.BlockSpec((tokens, cols), lambda i, m: (0, i))],
            out_specs=[
                pl.BlockSpec((slots, cols), lambda i, m: (0, i)),
                whole((slots, tokens)),
                whole((slots, tokens)),
            ],
        ),
        out_shape=[
            jax.ShapeDtypeStruct((slots, width), BF),
            jax.ShapeDtypeStruct((slots, tokens), BF),
            jax.ShapeDtypeStruct((slots, tokens), BF),
        ],
        compiler_params=params(16),
        name="dispatch",
    )(side, route_a.T, route_b.T, gates_a.T, gates_b.T, x)


def partial_kernel(side_ref, x_ref, w_ref, own_ref, s1_ref, s2_ref, s3_ref, *, cb):
    j = pl.program_id(0)
    part = dot(x_ref[...], w_ref[...], 1, cb)
    for step, ref in ((0, s1_ref), (1, s2_ref), (2, s3_ref)):

        @pl.when(j == step)
        def _(ref=ref):
            ref[...] = part.astype(BF)

    @pl.when(j == 3)
    def _():
        own_ref[...] = part


def partials(side, x, w, transposed):
    rows, depth = x.shape
    hid = (w.shape[0] if transposed else w.shape[1]) // 4
    if transposed:
        w_spec = pl.BlockSpec((hid, depth), lambda i, m: (m[0] ^ ((i + 1) % 4), 0))
    else:
        w_spec = pl.BlockSpec((depth, hid), lambda i, m: (0, m[0] ^ ((i + 1) % 4)))
    return pl.pallas_call(
        functools.partial(partial_kernel, cb=1 if transposed else 0),
        grid_spec=pltpu.PrefetchScalarGridSpec(
            num_scalar_prefetch=1,
            grid=(4,),
            in_specs=[whole((rows, depth)), w_spec],
            out_specs=[whole((rows, hid))] * 4,
        ),
        out_shape=[jax.ShapeDtypeStruct((rows, hid), F32)]
        + [jax.ShapeDtypeStruct((rows, hid), BF)] * 3,
        compiler_params=params(24),
        cost_estimate=pl.CostEstimate(
            flops=2 * rows * depth * hid * 4,
            bytes_accessed=2 * (rows * depth + 4 * depth * hid) + 10 * rows * hid,
            transcendentals=0,
        ),
        name="partials",
    )(side, x, w)


def merge_kernel(side_ref, a0_ref, a1_ref, a2_ref, a3_ref, w_ref, out_ref, *, transposed):
    total = None
    hid = a0_ref.shape[1]
    for j, ref in enumerate((a0_ref, a1_ref, a2_ref, a3_ref)):
        start = pl.multiple_of((side_ref[0] ^ j) * hid, hid)
        block = w_ref[:, pl.ds(start, hid)] if transposed else w_ref[pl.ds(start, hid), :]
        part = dot(ref[...], block, 1, 1 if transposed else 0)
        total = part if total is None else total + part
    out_ref[...] = total.astype(BF)


def merged(side, pieces, w, transposed):
    rows, hid = pieces[0].shape
    width = w.shape[0] if transposed else w.shape[1]
    cols = column_block(width)
    if transposed:
        w_spec = pl.BlockSpec((cols, 4 * hid), lambda i, m: (i, 0))
    else:
        w_spec = pl.BlockSpec((4 * hid, cols), lambda i, m: (0, i))
    return pl.pallas_call(
        functools.partial(merge_kernel, transposed=transposed),
        grid_spec=pltpu.PrefetchScalarGridSpec(
            num_scalar_prefetch=1,
            grid=(width // cols,),
            in_specs=[whole((rows, hid))] * 4 + [w_spec],
            out_specs=pl.BlockSpec((rows, cols), lambda i, m: (0, i)),
        ),
        out_shape=jax.ShapeDtypeStruct((rows, width), BF),
        compiler_params=params(24),
        cost_estimate=pl.CostEstimate(
            flops=2 * rows * width * hid * 4,
            bytes_accessed=2 * (rows * width + 4 * width * hid + 4 * rows * hid),
            transcendentals=0,
        ),
        name="merged",
    )(side, *pieces, w)


def weight_kernel(side_ref, a0_ref, a1_ref, a2_ref, a3_ref, d_ref, own_ref, send_ref, act_ref):
    hid = a0_ref.shape[1]

    @pl.when(pl.program_id(0) == 0)
    def _():
        for j, ref in enumerate((a0_ref, a1_ref, a2_ref, a3_ref)):
            start = pl.multiple_of((side_ref[0] ^ j) * hid, hid)
            act_ref[:, pl.ds(start, hid)] = ref[...]

    for half, ref in ((side_ref[1], own_ref), (1 - side_ref[1], send_ref)):
        act = act_ref[:, pl.ds(pl.multiple_of(half * (2 * hid), 2 * hid), 2 * hid)]
        ref[...] = dot(act, d_ref[...], 0, 0).astype(BF)


def weight_parts(side, pieces, d_out):
    rows, hid = pieces[0].shape
    width = d_out.shape[1]
    cols = column_block(width)
    return pl.pallas_call(
        weight_kernel,
        grid_spec=pltpu.PrefetchScalarGridSpec(
            num_scalar_prefetch=1,
            grid=(width // cols,),
            in_specs=[whole((rows, hid))] * 4 + [pl.BlockSpec((rows, cols), lambda i, m: (0, i))],
            out_specs=[pl.BlockSpec((2 * hid, cols), lambda i, m: (0, i))] * 2,
            scratch_shapes=[pltpu.VMEM((rows, 4 * hid), BF)],
        ),
        out_shape=[jax.ShapeDtypeStruct((2 * hid, width), BF)] * 2,
        compiler_params=params(24),
        cost_estimate=pl.CostEstimate(
            flops=2 * rows * width * hid * 4,
            bytes_accessed=2 * (rows * width + 4 * width * hid + 4 * rows * hid),
            transcendentals=0,
        ),
        name="weight_parts",
    )(side, *pieces, d_out)


def to_members(blocks):
    count = lax.axis_size("pipe")
    return [
        lax.ppermute(block, "pipe", [(p, p ^ (j + 1)) for p in range(count)])
        for j, block in enumerate(blocks)
    ]


def exchange(rows):
    experts = lax.axis_size("expert")
    blocks = rows.reshape(experts, CAP, -1)
    blocks = lax.all_to_all(blocks, "expert", split_axis=0, concat_axis=0, tiled=True)
    return blocks.reshape(experts * CAP, -1)


def shards(tokens, cotangent, route_a, route_b, gates_a, gates_b, w_up, w_down):
    pipe_size = lax.axis_size("pipe")
    half_size = pipe_size // 2
    slots = lax.axis_size("expert") * CAP
    pipe = lax.axis_index("pipe")
    side = jnp.stack([pipe % half_size, pipe // half_size]).astype(jnp.int32)
    up, down = w_up[0], w_down[0]

    sent_x, plain, gated = dispatch(side, route_a, route_b, gates_a, gates_b, tokens, slots)
    rows_x = exchange(sent_x)
    d_out = exchange(dot(gated, cotangent, 1, 0).astype(BF))

    own, *others = partials(side, rows_x, up, False)
    hidden = own + sum(block.astype(F32) for block in to_members(others))
    sigmoid = jax.nn.sigmoid(hidden)
    act = (hidden * sigmoid).astype(BF)
    acts = [act] + to_members([act] * 3)
    returned = exchange(merged(side, acts, down, False))

    own, *others = partials(side, d_out, down, True)
    d_act = own + sum(block.astype(F32) for block in to_members(others))
    d_hidden = (d_act * sigmoid * (1.0 + hidden * (1.0 - sigmoid))).astype(BF)
    d_hiddens = [d_hidden] + to_members([d_hidden] * 3)
    returned_dx = exchange(merged(side, d_hiddens, up, True))

    own_weight, travelling = weight_parts(side, acts, d_out)
    arrived = lax.ppermute(travelling, "pipe", [(p, pipe_size - 1 - p) for p in range(pipe_size)])
    grad_weight = (own_weight.astype(F32) + arrived.astype(F32)).astype(BF)

    layer_out = dot(gated, returned, 0, 0).astype(BF)
    grad_tokens = dot(plain, returned_dx, 0, 0).astype(BF)
    return (layer_out, grad_tokens, grad_weight[None])


def solution(mesh):
    in_specs = (
        P("expert", "pipe"),
        P("expert", "pipe"),
        P("expert", None),
        P("expert", None),
        P("expert", None),
        P("expert", None),
        P("expert", "pipe", None),
        P("expert", None, "pipe"),
    )
    out_specs = (P("expert", "pipe"), P("expert", "pipe"), P("expert", None, "pipe"))
    return jax.shard_map(shards, mesh=mesh, in_specs=in_specs, out_specs=out_specs, check_vma=False)
```

```python
import functools

import jax
import jax.numpy as jnp
from jax import lax
from jax.experimental import pallas as pl
from jax.experimental.pallas import tpu as pltpu
from jax.sharding import PartitionSpec as P

CAP = 16
BF = jnp.bfloat16
F32 = jnp.float32
RESIDENT = pl.BlockSpec(memory_space=pltpu.VMEM)
SCALARS = pl.BlockSpec(memory_space=pltpu.SMEM)
FAR = pl.BlockSpec(memory_space=pltpu.HBM)


def params():
    return pltpu.CompilerParams(vmem_limit_bytes=20 * 1024 * 1024)


def cost(flops, bytes_accessed):
    return pl.CostEstimate(flops=flops, bytes_accessed=bytes_accessed, transcendentals=0)


def near(array):
    return pltpu.with_memory_space_constraint(array, pltpu.VMEM)


def far(array):
    return pltpu.with_memory_space_constraint(array, pltpu.HBM)


def dot(a, b, ca, cb):
    return lax.dot_general(a, b, (((ca,), (cb,)), ((), ())), preferred_element_type=F32)


def column_block(width):
    for size in (256, 128):
        if width % size == 0:
            return size
    return width


def table_of(side_ref, ra_ref, rb_ref, ga_ref, gb_ref, expert_of, slots):
    upper = side_ref[1] == 1
    route = jnp.where(upper, rb_ref[...], ra_ref[...])
    gates = jnp.where(upper, gb_ref[...].astype(F32), ga_ref[...].astype(F32))
    top, tokens = route.shape
    experts = slots // CAP
    expert = lax.broadcasted_iota(jnp.int32, (experts, tokens), 0)
    member = jnp.zeros((experts, tokens), F32)
    gate = jnp.zeros((experts, tokens), F32)
    for k in range(top):
        named = route[k : k + 1, :] == expert
        member = member + jnp.where(named, 1.0, 0.0)
        gate = gate + jnp.where(named, gates[k : k + 1, :], 0.0)
    before = lax.broadcasted_iota(jnp.int32, (tokens, tokens), 0) < lax.broadcasted_iota(
        jnp.int32, (tokens, tokens), 1
    )
    earlier = dot(member.astype(BF), jnp.where(before, 1.0, 0.0).astype(BF), 1, 0)
    place = jnp.where(member > 0.5, earlier, 128.0).astype(BF)
    row = lax.broadcasted_iota(jnp.int32, (slots, experts), 0)
    column = lax.broadcasted_iota(jnp.int32, (slots, experts), 1)
    spread = jnp.where(expert_of(row // CAP) == column, 1.0, 0.0).astype(BF)
    place_rows = dot(spread, place, 1, 0)
    gate_rows = dot(spread, gate.astype(BF), 1, 0)
    slot = lax.broadcasted_iota(jnp.int32, (slots, tokens), 0) % CAP
    hit = place_rows == slot.astype(F32)
    return jnp.where(hit, 1.0, 0.0).astype(BF), jnp.where(hit, gate_rows, 0.0).astype(BF)


def fetch(source, target, sems, axis, parts):
    size = source.shape[axis] // parts
    copies = []
    for i in range(parts):
        span = tuple(pl.ds(i * size, size) if d == axis else slice(None) for d in range(2))
        copies.append(pltpu.make_async_copy(source.at[span], target.at[span], sems.at[i]))
    return copies


def streamed(source, target, sems, cols):
    step = pl.program_id(0)

    @pl.when(step == 0)
    def _():
        for copy in fetch(source, target, sems, 1, source.shape[1] // cols):
            copy.start()

    span = (slice(None), pl.ds(pl.multiple_of(step * cols, cols), cols))
    pltpu.make_async_copy(source.at[span], target.at[span], sems.at[step]).wait()
    return target[span]


def dispatch_kernel(side_ref, ra_ref, rb_ref, ga_ref, gb_ref, x_ref, *refs, depth, count):
    outs, flipped, (table_ref, x_all, out_all, sem, sems) = refs[:count], refs[count:-5], refs[-5:]
    routing = (side_ref, ra_ref, rb_ref, ga_ref, gb_ref)
    copy = pltpu.make_async_copy(x_ref, x_all, sem)

    def by_depth(block):
        return block // 2 % 2 * (2 * depth) + block // 4 * 2 + block % 2

    def by_plane(block):
        flip_x, flip_core = block // (2 * depth), block // depth % 2
        return (side_ref[2] ^ flip_x) * (2 * depth) + block % depth * 2 + (side_ref[3] ^ flip_core)

    copy.start()
    slots = table_ref.shape[0]
    if count == 1:
        table_ref[...] = table_of(*routing, by_depth, slots)[0]
    else:
        table_ref[...] = table_of(*routing, by_plane, slots)[1]
        for ref, table in zip(flipped, table_of(*routing, by_depth, slots)):
            ref[...] = table.T
    copy.wait()
    height, width = outs[0].shape
    cols = column_block(width)
    copies = []
    for k in range(width // cols):
        span = slice(k * cols, (k + 1) * cols)
        out_all[:, span] = dot(table_ref[...], x_all[:, span], 1, 0).astype(BF)
        for i, out_ref in enumerate(outs):
            source = out_all.at[i * height : (i + 1) * height, span]
            copies.append(pltpu.make_async_copy(source, out_ref.at[:, span], sems.at[len(copies)]))
            copies[-1].start()
    for copy in copies:
        copy.wait()


def dispatch(side, routing, x, slots, depth, count):
    tokens, width = x.shape
    tables = 0 if count == 1 else 2
    return pl.pallas_call(
        functools.partial(dispatch_kernel, depth=depth, count=count),
        in_specs=[SCALARS] + [RESIDENT] * 4 + [FAR],
        out_specs=[FAR] * count + [RESIDENT] * tables,
        out_shape=[pltpu.HBM((slots // count, width), BF)] * count
        + [jax.ShapeDtypeStruct((tokens, slots), BF)] * tables,
        scratch_shapes=[
            pltpu.VMEM((slots, tokens), BF),
            pltpu.VMEM((tokens, width), BF),
            pltpu.VMEM((slots, width), BF),
            pltpu.SemaphoreType.DMA,
            pltpu.SemaphoreType.DMA((count * (width // column_block(width)),)),
        ],
        compiler_params=params(),
        cost_estimate=cost(2 * slots * tokens * width, 2 * (slots + tokens) * width),
        name="dispatch",
    )(side, *[far(array) for array in routing], far(x))


def regroup_kernel(side_ref, *refs, members):
    pieces, (out_ref, held, sems) = refs[: len(members)], refs[-3:]
    arriving = [pltpu.make_async_copy(ref, held.at[i], sems.at[i]) for i, ref in enumerate(pieces)]
    leaving = []
    for copy in arriving:
        copy.start()
    for i, (j, copy) in enumerate(zip(members, arriving)):
        place = (side_ref[2] ^ (j // 2)) * 2 + (side_ref[3] ^ (j % 2))
        copy.wait()
        leaving.append(pltpu.make_async_copy(held.at[i], out_ref.at[:, place], sems.at[len(members) + i]))
        leaving[-1].start()
    for copy in leaving:
        copy.wait()


def regroup(side, pieces, depth, members, base=None):
    width = pieces[0].shape[1]
    pieces = [far(piece.reshape(depth, CAP, width)) for piece in pieces]
    more = [] if base is None else [far(base)]
    return pl.pallas_call(
        functools.partial(regroup_kernel, members=members),
        in_specs=[SCALARS] + [FAR] * (len(pieces) + len(more)),
        out_specs=FAR,
        out_shape=pltpu.HBM((depth, 4, CAP, width), BF),
        scratch_shapes=[
            pltpu.VMEM((len(members), depth, CAP, width), BF),
            pltpu.SemaphoreType.DMA((2 * len(members),)),
        ],
        input_output_aliases={1 + len(pieces): 0} if more else {},
        compiler_params=params(),
        cost_estimate=cost(0, 4 * CAP * depth * width * len(members)),
        name="regroup",
    )(side, *pieces, *more)


def hold_kernel(source, target, sems):
    copies = fetch(source, target, sems, 0, 4)
    for copy in copies:
        copy.start()
    for copy in copies:
        copy.wait()


def hold(weight):
    return pl.pallas_call(
        hold_kernel,
        in_specs=[FAR],
        out_specs=RESIDENT,
        out_shape=pltpu.VMEM(weight.shape, BF),
        scratch_shapes=[pltpu.SemaphoreType.DMA((4,))],
        compiler_params=params(),
        cost_estimate=cost(0, 4 * weight.size),
        name="hold",
    )(far(weight))


def partial_kernel(side_ref, x_ref, w_ref, own_ref, s1_ref, s2_ref, s3_ref, *refs, transposed):
    *kept, own_all, sent_all, sems = refs
    hid = own_ref.shape[1]
    copies = [pltpu.make_async_copy(x_ref, ref, sems.at[4]) for ref in kept]
    for copy in copies:
        copy.start()
    for j, ref in ((3, s3_ref), (1, s1_ref), (2, s2_ref), (0, own_ref)):
        block = pl.ds(pl.multiple_of((side_ref[0] ^ j) * hid, hid), hid)
        weight = w_ref[block, :] if transposed else w_ref[:, block]
        part = dot(x_ref[...], weight, 1, 1 if transposed else 0)
        held = sent_all.at[j - 1] if ref.dtype == BF else own_all.at[j]
        held[...] = part.astype(ref.dtype)
        copies.append(pltpu.make_async_copy(held, ref, sems.at[j]))
        copies[-1].start()
    for copy in copies:
        copy.wait()


def partials(side, x, w, transposed):
    rows, depth = x.shape
    hid = (w.shape[0] if transposed else w.shape[1]) // 4
    shapes = [pltpu.HBM((rows, hid), F32)] + [pltpu.HBM((rows, hid), BF)] * 3
    if transposed:
        shapes[1] = shapes[0]
        shapes.append(pltpu.HBM(x.shape, BF))
    return pl.pallas_call(
        functools.partial(partial_kernel, transposed=transposed),
        in_specs=[SCALARS, RESIDENT, RESIDENT],
        out_specs=[FAR] * len(shapes),
        out_shape=shapes,
        scratch_shapes=[
            pltpu.VMEM((2, rows, hid), F32),
            pltpu.VMEM((3, rows, hid), BF),
            pltpu.SemaphoreType.DMA((5,)),
        ],
        compiler_params=params(),
        cost_estimate=cost(8 * rows * depth * hid, 2 * (rows * depth + 4 * depth * hid) + 10 * rows * hid),
        name="partials",
    )(side, near(x), near(w))


def merge_kernel(side_ref, a0_ref, a1_ref, a2_ref, a3_ref, w_ref, out_ref, *refs, transposed):
    *flipped_ref, out_all, flipped, sems = refs
    pieces = (a0_ref, a1_ref, a2_ref, a3_ref)
    rows, hid = a0_ref.shape
    width = out_all.shape[1]
    cols = column_block(width)
    blocks = [pl.ds(pl.multiple_of((side_ref[0] ^ j) * hid, hid), hid) for j in range(4)]
    copies = []
    for i in range(width // cols):
        span = slice(i * cols, (i + 1) * cols)
        total = None
        for ref, block in zip(pieces, blocks):
            if transposed:
                part = dot(ref[...], w_ref[span, block], 1, 1)
            else:
                part = dot(ref[...], w_ref[block, span], 1, 0)
            total = part if total is None else total + part
        out_all[:, span] = total.astype(BF)
        copies.append(pltpu.make_async_copy(out_all.at[:, span], out_ref.at[:, span], sems.at[i]))
        copies[-1].start()
    if flipped_ref:
        for ref, block in zip(pieces, blocks):
            flipped[block, :] = ref[...].T
        copies.append(pltpu.make_async_copy(flipped, flipped_ref[0], sems.at[width // cols]))
        copies[-1].start()
    for copy in copies:
        copy.wait()


def merged(side, pieces, w, transposed):
    rows, hid = pieces[0].shape
    width = w.shape[0] if transposed else w.shape[1]
    shapes = [pltpu.HBM((rows, width), BF)]
    if not transposed:
        shapes.append(pltpu.HBM((4 * hid, rows), BF))
    return pl.pallas_call(
        functools.partial(merge_kernel, transposed=transposed),
        in_specs=[SCALARS] + [RESIDENT] * 5,
        out_specs=[FAR] * len(shapes),
        out_shape=shapes,
        scratch_shapes=[
            pltpu.VMEM((rows, width), BF),
            pltpu.VMEM((4 * hid, rows), BF),
            pltpu.SemaphoreType.DMA((width // column_block(width) + 1,)),
        ],
        compiler_params=params(),
        cost_estimate=cost(8 * rows * width * hid, 2 * (rows * width + 4 * width * hid + 4 * rows * hid)),
        name="merged",
    )(side, *pieces, near(w))


def weight_kernel(side_ref, act_ref, d_ref, first_ref, rest_ref, own_ref, d_all, sems):
    rows, cols = own_ref.shape
    early = first_ref.shape[0]
    d_out = streamed(d_ref, d_all, sems, cols)
    own = act_ref[pl.ds(pl.multiple_of(side_ref[1] * rows, rows), rows), :]
    other = act_ref[pl.ds(pl.multiple_of((1 - side_ref[1]) * rows, rows), rows), :]
    sent = dot(other, d_out, 1, 0).astype(BF)
    first_ref[...] = sent[:early]
    rest_ref[...] = sent[early:]
    own_ref[...] = dot(own, d_out, 1, 0).astype(BF)


def weight_parts(side, acts, d_out, early):
    hid, rows = acts.shape
    width = d_out.shape[1]
    cols = column_block(width)
    heights = (early, hid // 2 - early, hid // 2)
    return pl.pallas_call(
        weight_kernel,
        grid=(width // cols,),
        in_specs=[SCALARS, pl.BlockSpec((hid, rows), lambda i: (0, 0)), FAR],
        out_specs=[pl.BlockSpec((height, cols), lambda i: (0, i)) for height in heights],
        out_shape=[pltpu.HBM((height, width), BF) for height in heights],
        scratch_shapes=[pltpu.VMEM((rows, width), BF), pltpu.SemaphoreType.DMA((width // cols,))],
        compiler_params=params(),
        cost_estimate=cost(2 * rows * width * hid, 2 * (rows * width + width * hid + rows * hid)),
        name="weight_parts",
    )(side, far(acts), far(d_out))


def combine_kernel(table_ref, x_ref, *refs, kept):
    if kept:
        next_ref, out_ref, next_out, out_all, sems = refs
    else:
        out_ref, out_all, sems = refs
    copies = []
    tokens, width = out_all.shape
    cols = column_block(width)
    for i in range(width // cols):
        span = (slice(None), slice(i * cols, (i + 1) * cols))
        out_all[span] = dot(table_ref[...], x_ref[span], 1, 0).astype(BF)
        copies.append(pltpu.make_async_copy(out_all.at[span], out_ref.at[span], sems.at[i]))
        copies[-1].start()
    if kept:
        next_out[...] = next_ref[...]
    for copy in copies:
        copy.wait()


def combine(table, rows, following=None):
    tokens, slots = table.shape
    width = rows.shape[1]
    kept = following is not None
    return pl.pallas_call(
        functools.partial(combine_kernel, kept=kept),
        in_specs=[RESIDENT] * (3 if kept else 2),
        out_specs=[FAR] + [RESIDENT] * kept,
        out_shape=[pltpu.HBM((tokens, width), BF)] + [pltpu.VMEM(table.shape, BF)] * kept,
        scratch_shapes=[pltpu.VMEM((tokens, width), BF), pltpu.SemaphoreType.DMA((width // column_block(width),))],
        compiler_params=params(),
        cost_estimate=cost(2 * slots * tokens * width, 2 * (slots + tokens) * width),
        name="combine",
    )(*((table, rows, following) if kept else (near(table), near(rows))))


def to_member(block, flip):
    count = lax.axis_size("pipe")
    return lax.ppermute(block, "pipe", [(p, p ^ flip) for p in range(count)])


def to_members(blocks):
    return [to_member(block, j + 1) for j, block in enumerate(blocks)]


def to_mirror(block):
    count = lax.axis_size("pipe")
    return lax.ppermute(block, "pipe", [(p, count - 1 - p) for p in range(count)])


def exchange(rows, groups):
    ranks = len(groups[0])
    blocks = rows.reshape(ranks, rows.shape[0] // ranks, -1)
    blocks = lax.all_to_all(
        blocks, "expert", split_axis=0, concat_axis=0, tiled=True, axis_index_groups=groups
    )
    return blocks.reshape(rows.shape)


def shards(tokens, cotangent, route_a, route_b, gates_a, gates_b, w_up, w_down):
    half_size = lax.axis_size("pipe") // 2
    experts = lax.axis_size("expert")
    slots, depth = experts * CAP, experts // 4
    up, down = w_up[0], w_down[0]
    pipe, expert = lax.axis_index("pipe"), lax.axis_index("expert")
    side = [pipe % half_size, pipe // half_size, expert // (2 * depth), expert % 2]
    side = jnp.stack(side).astype(jnp.int32)
    columns = [[(x * depth + z) * 2 + core for z in range(depth)] for x in range(2) for core in range(2)]
    everyone = [[column[z] for z in range(depth) for column in columns]]

    routing = [route_a.T, route_b.T, gates_a.T, gates_b.T]
    (sent_x,) = dispatch(side, routing, tokens, slots, depth, 1)
    rows_x = exchange(sent_x, everyone)
    *pieces, plain_flipped, gated_flipped = dispatch(side, routing, cotangent, slots, depth, 4)
    for j in range(1, 4):
        flip = j // 2 * (2 * depth) + j % 2
        pieces[j] = lax.ppermute(pieces[j], "expert", [(e, e ^ flip) for e in range(experts)])
    grouped = regroup(side, pieces[:3], depth, (0, 1, 2))
    grouped = regroup(side, pieces[3:], depth, (3,), grouped).reshape(slots, -1)

    grouped, rows_x = lax.optimization_barrier((grouped, rows_x))
    d_out = exchange(grouped, columns)
    own, *others = partials(side, rows_x, up, False)
    hidden = own + sum(block.astype(F32) for block in to_members(others))
    sigmoid = jax.nn.sigmoid(hidden)
    act = (hidden * sigmoid).astype(BF)
    act, down = lax.optimization_barrier((act, down))
    down_held = hold(down)
    acts = [act] + to_members([act] * 3)
    result, acts_flipped = merged(side, acts, down_held, False)
    result, d_out = lax.optimization_barrier((result, d_out))

    own, beside, far_off, diagonal, d_out = partials(side, d_out, down, True)
    result, own, beside, far_off, diagonal, d_out = lax.optimization_barrier(
        (result, own, beside, far_off, diagonal, d_out)
    )
    returned = exchange(result, everyone)
    diagonal = to_member(diagonal, 2)
    far_off = to_member(far_off, 2)
    beside = to_member((beside + diagonal.astype(F32)).astype(BF), 1)
    first, rest, own_weight = weight_parts(side, acts_flipped, d_out, slots // 8 * 3)
    d_act = own + far_off.astype(F32) + beside.astype(F32)
    d_hidden = (d_act * sigmoid * (1.0 + hidden * (1.0 - sigmoid))).astype(BF)
    d_hidden, first, rest, up = lax.optimization_barrier((d_hidden, first, rest, up))
    beside = to_member(d_hidden, 1)
    far_off = to_member(d_hidden, 2)
    up_held = hold(up)
    beside, far_off, first = lax.optimization_barrier((beside, far_off, first))
    d_hiddens = [d_hidden, beside, far_off, to_member(beside, 2)]
    first = to_mirror(first)
    (d_rows,) = merged(side, d_hiddens, up_held, True)
    d_rows, returned, first = lax.optimization_barrier((d_rows, returned, first))
    returned_dx = exchange(d_rows, everyone)
    rest = to_mirror(rest)

    layer_out, plain_held = combine(gated_flipped, returned, plain_flipped)
    layer_out, rest = lax.optimization_barrier((layer_out, rest))
    arrived = jnp.concatenate([first, rest])
    grad_weight = (own_weight.astype(F32) + arrived.astype(F32)).astype(BF)
    (grad_tokens,) = combine(plain_held, returned_dx)
    return (layer_out, grad_tokens, grad_weight[None])


def solution(mesh):
    in_specs = (
        P("expert", "pipe"),
        P("expert", "pipe"),
        P("expert", None),
        P("expert", None),
        P("expert", None),
        P("expert", None),
        P("expert", "pipe", None),
        P("expert", None, "pipe"),
    )
    out_specs = (P("expert", "pipe"), P("expert", "pipe"), P("expert", None, "pipe"))
    return jax.shard_map(shards, mesh=mesh, in_specs=in_specs, out_specs=out_specs, check_vma=False)
```

```python
import functools

import jax
import jax.numpy as jnp
from jax import lax
from jax.experimental import pallas as pl
from jax.experimental.pallas import tpu as pltpu
from jax.sharding import PartitionSpec as P

CAP = 16
BF = jnp.bfloat16
F32 = jnp.float32
RESIDENT = pl.BlockSpec(memory_space=pltpu.VMEM)
SCALARS = pl.BlockSpec(memory_space=pltpu.SMEM)
FAR = pl.BlockSpec(memory_space=pltpu.HBM)


def params():
    return pltpu.CompilerParams(vmem_limit_bytes=20 * 1024 * 1024)


def cost(flops, bytes_accessed):
    return pl.CostEstimate(flops=flops, bytes_accessed=bytes_accessed, transcendentals=0)


def near(array):
    return pltpu.with_memory_space_constraint(array, pltpu.VMEM)


def far(array):
    return pltpu.with_memory_space_constraint(array, pltpu.HBM)


def dot(a, b, ca, cb):
    return lax.dot_general(a, b, (((ca,), (cb,)), ((), ())), preferred_element_type=F32)


def column_block(width):
    for size in (256, 128):
        if width % size == 0:
            return size
    return width


def table_of(side_ref, ra_ref, rb_ref, ga_ref, gb_ref, expert_of, slots):
    upper = side_ref[1] == 1
    route = jnp.where(upper, rb_ref[...], ra_ref[...])
    gates = jnp.where(upper, gb_ref[...].astype(F32), ga_ref[...].astype(F32))
    top, tokens = route.shape
    experts = slots // CAP
    expert = lax.broadcasted_iota(jnp.int32, (experts, tokens), 0)
    member = jnp.zeros((experts, tokens), F32)
    gate = jnp.zeros((experts, tokens), F32)
    for k in range(top):
        named = route[k : k + 1, :] == expert
        member = member + jnp.where(named, 1.0, 0.0)
        gate = gate + jnp.where(named, gates[k : k + 1, :], 0.0)
    before = lax.broadcasted_iota(jnp.int32, (tokens, tokens), 0) < lax.broadcasted_iota(
        jnp.int32, (tokens, tokens), 1
    )
    earlier = dot(member.astype(BF), jnp.where(before, 1.0, 0.0).astype(BF), 1, 0)
    place = jnp.where(member > 0.5, earlier, 128.0).astype(BF)
    row = lax.broadcasted_iota(jnp.int32, (slots, experts), 0)
    column = lax.broadcasted_iota(jnp.int32, (slots, experts), 1)
    spread = jnp.where(expert_of(row // CAP) == column, 1.0, 0.0).astype(BF)
    place_rows = dot(spread, place, 1, 0)
    gate_rows = dot(spread, gate.astype(BF), 1, 0)
    slot = lax.broadcasted_iota(jnp.int32, (slots, tokens), 0) % CAP
    hit = place_rows == slot.astype(F32)
    return jnp.where(hit, 1.0, 0.0).astype(BF), jnp.where(hit, gate_rows, 0.0).astype(BF)


def fetch(source, target, sems, axis, parts):
    size = source.shape[axis] // parts
    copies = []
    for i in range(parts):
        span = tuple(pl.ds(i * size, size) if d == axis else slice(None) for d in range(2))
        copies.append(pltpu.make_async_copy(source.at[span], target.at[span], sems.at[i]))
    return copies


def streamed(source, target, sems, cols):
    step = pl.program_id(0)

    @pl.when(step == 0)
    def _():
        for copy in fetch(source, target, sems, 1, source.shape[1] // cols):
            copy.start()

    span = (slice(None), pl.ds(pl.multiple_of(step * cols, cols), cols))
    pltpu.make_async_copy(source.at[span], target.at[span], sems.at[step]).wait()
    return target[span]


def dispatch_kernel(side_ref, ra_ref, rb_ref, ga_ref, gb_ref, x_ref, *refs, depth, count):
    outs, flipped, (table_ref, x_all, out_all, sem, sems) = refs[:count], refs[count:-5], refs[-5:]
    routing = (side_ref, ra_ref, rb_ref, ga_ref, gb_ref)
    copy = pltpu.make_async_copy(x_ref, x_all, sem)

    def by_depth(block):
        return block // 2 % 2 * (2 * depth) + block // 4 * 2 + block % 2

    def by_plane(block):
        flip_x, flip_core = block // (2 * depth), block // depth % 2
        return (side_ref[2] ^ flip_x) * (2 * depth) + block % depth * 2 + (side_ref[3] ^ flip_core)

    copy.start()
    slots = table_ref.shape[0]
    if count == 1:
        table_ref[...] = table_of(*routing, by_depth, slots)[0]
    else:
        table_ref[...] = table_of(*routing, by_plane, slots)[1]
        for ref, table in zip(flipped, table_of(*routing, by_depth, slots)):
            ref[...] = table.T
    copy.wait()
    height, width = outs[0].shape
    cols = column_block(width)
    copies = []
    for k in range(width // cols):
        span = slice(k * cols, (k + 1) * cols)
        out_all[:, span] = dot(table_ref[...], x_all[:, span], 1, 0).astype(BF)
        for i, out_ref in enumerate(outs):
            source = out_all.at[i * height : (i + 1) * height, span]
            copies.append(pltpu.make_async_copy(source, out_ref.at[:, span], sems.at[len(copies)]))
            copies[-1].start()
    for copy in copies:
        copy.wait()


def dispatch(side, routing, x, slots, depth, count):
    tokens, width = x.shape
    tables = 0 if count == 1 else 2
    return pl.pallas_call(
        functools.partial(dispatch_kernel, depth=depth, count=count),
        in_specs=[SCALARS] + [RESIDENT] * 4 + [FAR],
        out_specs=[FAR] * count + [RESIDENT] * tables,
        out_shape=[pltpu.HBM((slots // count, width), BF)] * count
        + [jax.ShapeDtypeStruct((tokens, slots), BF)] * tables,
        scratch_shapes=[
            pltpu.VMEM((slots, tokens), BF),
            pltpu.VMEM((tokens, width), BF),
            pltpu.VMEM((slots, width), BF),
            pltpu.SemaphoreType.DMA,
            pltpu.SemaphoreType.DMA((count * (width // column_block(width)),)),
        ],
        compiler_params=params(),
        cost_estimate=cost(2 * slots * tokens * width, 2 * (slots + tokens) * width),
        name="dispatch",
    )(side, *[far(array) for array in routing], far(x))


def regroup_kernel(side_ref, *refs, members):
    pieces, (out_ref, held, sems) = refs[: len(members)], refs[-3:]
    arriving = [pltpu.make_async_copy(ref, held.at[i], sems.at[i]) for i, ref in enumerate(pieces)]
    leaving = []
    for copy in arriving:
        copy.start()
    for i, (j, copy) in enumerate(zip(members, arriving)):
        place = (side_ref[2] ^ (j // 2)) * 2 + (side_ref[3] ^ (j % 2))
        copy.wait()
        leaving.append(pltpu.make_async_copy(held.at[i], out_ref.at[:, place], sems.at[len(members) + i]))
        leaving[-1].start()
    for copy in leaving:
        copy.wait()


def regroup(side, pieces, depth, members, base=None):
    width = pieces[0].shape[1]
    pieces = [far(piece.reshape(depth, CAP, width)) for piece in pieces]
    more = [] if base is None else [far(base)]
    return pl.pallas_call(
        functools.partial(regroup_kernel, members=members),
        in_specs=[SCALARS] + [FAR] * (len(pieces) + len(more)),
        out_specs=FAR,
        out_shape=pltpu.HBM((depth, 4, CAP, width), BF),
        scratch_shapes=[
            pltpu.VMEM((len(members), depth, CAP, width), BF),
            pltpu.SemaphoreType.DMA((2 * len(members),)),
        ],
        input_output_aliases={1 + len(pieces): 0} if more else {},
        compiler_params=params(),
        cost_estimate=cost(0, 4 * CAP * depth * width * len(members)),
        name="regroup",
    )(side, *pieces, *more)


def hold_kernel(source, target, sems):
    copies = fetch(source, target, sems, 0, 4)
    for copy in copies:
        copy.start()
    for copy in copies:
        copy.wait()


def hold(weight):
    return pl.pallas_call(
        hold_kernel,
        in_specs=[FAR],
        out_specs=RESIDENT,
        out_shape=pltpu.VMEM(weight.shape, BF),
        scratch_shapes=[pltpu.SemaphoreType.DMA((4,))],
        compiler_params=params(),
        cost_estimate=cost(0, 4 * weight.size),
        name="hold",
    )(far(weight))


def partial_kernel(side_ref, x_ref, w_ref, own_ref, s1_ref, s2_ref, s3_ref, *refs, transposed):
    *kept, own_all, sent_all, sems = refs
    hid = own_ref.shape[1]
    copies = [pltpu.make_async_copy(x_ref, ref, sems.at[4]) for ref in kept]
    for copy in copies:
        copy.start()
    for j, ref in ((3, s3_ref), (1, s1_ref), (2, s2_ref), (0, own_ref)):
        block = pl.ds(pl.multiple_of((side_ref[0] ^ j) * hid, hid), hid)
        weight = w_ref[block, :] if transposed else w_ref[:, block]
        part = dot(x_ref[...], weight, 1, 1 if transposed else 0)
        held = sent_all.at[j - 1] if ref.dtype == BF else own_all.at[j]
        held[...] = part.astype(ref.dtype)
        copies.append(pltpu.make_async_copy(held, ref, sems.at[j]))
        copies[-1].start()
    for copy in copies:
        copy.wait()


def partials(side, x, w, transposed):
    rows, depth = x.shape
    hid = (w.shape[0] if transposed else w.shape[1]) // 4
    shapes = [pltpu.HBM((rows, hid), F32)] + [pltpu.HBM((rows, hid), BF)] * 3
    if transposed:
        shapes[1] = shapes[0]
        shapes.append(pltpu.HBM(x.shape, BF))
    return pl.pallas_call(
        functools.partial(partial_kernel, transposed=transposed),
        in_specs=[SCALARS, RESIDENT, RESIDENT],
        out_specs=[FAR] * len(shapes),
        out_shape=shapes,
        scratch_shapes=[
            pltpu.VMEM((2, rows, hid), F32),
            pltpu.VMEM((3, rows, hid), BF),
            pltpu.SemaphoreType.DMA((5,)),
        ],
        compiler_params=params(),
        cost_estimate=cost(8 * rows * depth * hid, 2 * (rows * depth + 4 * depth * hid) + 10 * rows * hid),
        name="partials",
    )(side, near(x), near(w))


def merge_kernel(side_ref, a0_ref, a1_ref, a2_ref, a3_ref, w_ref, out_ref, *refs, transposed):
    *flipped_ref, out_all, flipped, sems = refs
    pieces = (a0_ref, a1_ref, a2_ref, a3_ref)
    rows, hid = a0_ref.shape
    width = out_all.shape[1]
    cols = column_block(width)
    blocks = [pl.ds(pl.multiple_of((side_ref[0] ^ j) * hid, hid), hid) for j in range(4)]
    copies = []
    for i in range(width // cols):
        span = slice(i * cols, (i + 1) * cols)
        total = None
        for ref, block in zip(pieces, blocks):
            if transposed:
                part = dot(ref[...], w_ref[span, block], 1, 1)
            else:
                part = dot(ref[...], w_ref[block, span], 1, 0)
            total = part if total is None else total + part
        out_all[:, span] = total.astype(BF)
        copies.append(pltpu.make_async_copy(out_all.at[:, span], out_ref.at[:, span], sems.at[i]))
        copies[-1].start()
    if flipped_ref:
        for ref, block in zip(pieces, blocks):
            flipped[block, :] = ref[...].T
        copies.append(pltpu.make_async_copy(flipped, flipped_ref[0], sems.at[width // cols]))
        copies[-1].start()
    for copy in copies:
        copy.wait()


def merged(side, pieces, w, transposed):
    rows, hid = pieces[0].shape
    width = w.shape[0] if transposed else w.shape[1]
    shapes = [pltpu.HBM((rows, width), BF)]
    if not transposed:
        shapes.append(pltpu.HBM((4 * hid, rows), BF))
    return pl.pallas_call(
        functools.partial(merge_kernel, transposed=transposed),
        in_specs=[SCALARS] + [RESIDENT] * 5,
        out_specs=[FAR] * len(shapes),
        out_shape=shapes,
        scratch_shapes=[
            pltpu.VMEM((rows, width), BF),
            pltpu.VMEM((4 * hid, rows), BF),
            pltpu.SemaphoreType.DMA((width // column_block(width) + 1,)),
        ],
        compiler_params=params(),
        cost_estimate=cost(8 * rows * width * hid, 2 * (rows * width + 4 * width * hid + 4 * rows * hid)),
        name="merged",
    )(side, *pieces, near(w))


def weight_kernel(side_ref, act_ref, d_ref, first_ref, rest_ref, own_ref, d_all, sems):
    rows, cols = own_ref.shape
    early = first_ref.shape[0]
    d_out = streamed(d_ref, d_all, sems, cols)
    own = act_ref[pl.ds(pl.multiple_of(side_ref[1] * rows, rows), rows), :]
    other = act_ref[pl.ds(pl.multiple_of((1 - side_ref[1]) * rows, rows), rows), :]
    sent = dot(other, d_out, 1, 0).astype(BF)
    first_ref[...] = sent[:early]
    rest_ref[...] = sent[early:]
    own_ref[...] = dot(own, d_out, 1, 0).astype(BF)


def weight_parts(side, acts, d_out, early):
    hid, rows = acts.shape
    width = d_out.shape[1]
    cols = column_block(width)
    heights = (early, hid // 2 - early, hid // 2)
    return pl.pallas_call(
        weight_kernel,
        grid=(width // cols,),
        in_specs=[SCALARS, pl.BlockSpec((hid, rows), lambda i: (0, 0)), FAR],
        out_specs=[pl.BlockSpec((height, cols), lambda i: (0, i)) for height in heights],
        out_shape=[pltpu.HBM((height, width), BF) for height in heights],
        scratch_shapes=[pltpu.VMEM((rows, width), BF), pltpu.SemaphoreType.DMA((width // cols,))],
        compiler_params=params(),
        cost_estimate=cost(2 * rows * width * hid, 2 * (rows * width + width * hid + rows * hid)),
        name="weight_parts",
    )(side, far(acts), far(d_out))


def combine_kernel(*refs, count, kept):
    table_ref, parts, refs = refs[0], refs[1 : count + 1], refs[count + 1 :]
    if kept:
        next_ref, out_ref, next_out, out_all, sems = refs
    else:
        out_ref, out_all, sems = refs
    copies = []
    tokens, width = out_all.shape
    cols, rows = column_block(width), parts[0].shape[0]
    for i in range(width // cols):
        span = (slice(None), slice(i * cols, (i + 1) * cols))
        total = None
        for k, ref in enumerate(parts):
            part = dot(table_ref[:, k * rows : (k + 1) * rows], ref[span], 1, 0)
            total = part if total is None else total + part
        out_all[span] = total.astype(BF)
        copies.append(pltpu.make_async_copy(out_all.at[span], out_ref.at[span], sems.at[i]))
        copies[-1].start()
    if kept:
        next_out[...] = next_ref[...]
    for copy in copies:
        copy.wait()


def combine(table, parts, following=None):
    tokens, slots = table.shape
    width = parts[0].shape[1]
    kept = following is not None
    return pl.pallas_call(
        functools.partial(combine_kernel, count=len(parts), kept=kept),
        in_specs=[RESIDENT] * (1 + len(parts) + kept),
        out_specs=[FAR] + [RESIDENT] * kept,
        out_shape=[pltpu.HBM((tokens, width), BF)] + [pltpu.VMEM(table.shape, BF)] * kept,
        scratch_shapes=[pltpu.VMEM((tokens, width), BF), pltpu.SemaphoreType.DMA((width // column_block(width),))],
        compiler_params=params(),
        cost_estimate=cost(2 * slots * tokens * width, 2 * (slots + tokens) * width),
        name="combine",
    )(*((table, *parts, following) if kept else (near(table), *[near(part) for part in parts])))


def to_member(block, flip):
    count = lax.axis_size("pipe")
    return lax.ppermute(block, "pipe", [(p, p ^ flip) for p in range(count)])


def to_members(blocks):
    return [to_member(block, j + 1) for j, block in enumerate(blocks)]


def to_mirror(block):
    count = lax.axis_size("pipe")
    return lax.ppermute(block, "pipe", [(p, count - 1 - p) for p in range(count)])


def exchange(rows, groups):
    ranks = len(groups[0])
    blocks = rows.reshape(ranks, rows.shape[0] // ranks, -1)
    blocks = lax.all_to_all(
        blocks, "expert", split_axis=0, concat_axis=0, tiled=True, axis_index_groups=groups
    )
    return blocks.reshape(rows.shape)


def shards(tokens, cotangent, route_a, route_b, gates_a, gates_b, w_up, w_down):
    half_size = lax.axis_size("pipe") // 2
    experts = lax.axis_size("expert")
    slots, depth = experts * CAP, experts // 4
    up, down = w_up[0], w_down[0]
    pipe, expert = lax.axis_index("pipe"), lax.axis_index("expert")
    side = [pipe % half_size, pipe // half_size, expert // (2 * depth), expert % 2]
    side = jnp.stack(side).astype(jnp.int32)
    columns = [[(x * depth + z) * 2 + core for z in range(depth)] for x in range(2) for core in range(2)]
    everyone = [[column[z] for z in range(depth) for column in columns]]

    routing = [route_a.T, route_b.T, gates_a.T, gates_b.T]
    (sent_x,) = dispatch(side, routing, tokens, slots, depth, 1)
    rows_x = exchange(sent_x, everyone)
    *pieces, plain_flipped, gated_flipped = dispatch(side, routing, cotangent, slots, depth, 4)
    for j in range(1, 4):
        flip = j // 2 * (2 * depth) + j % 2
        pieces[j] = lax.ppermute(pieces[j], "expert", [(e, e ^ flip) for e in range(experts)])
    grouped = regroup(side, pieces[:3], depth, (0, 1, 2))
    grouped = regroup(side, pieces[3:], depth, (3,), grouped).reshape(slots, -1)

    grouped, rows_x = lax.optimization_barrier((grouped, rows_x))
    d_out = exchange(grouped, columns)
    own, *others = partials(side, rows_x, up, False)
    hidden = own + sum(block.astype(F32) for block in to_members(others))
    sigmoid = jax.nn.sigmoid(hidden)
    act = (hidden * sigmoid).astype(BF)
    act, down = lax.optimization_barrier((act, down))
    down_held = hold(down)
    acts = [act] + to_members([act] * 3)
    result, acts_flipped = merged(side, acts, down_held, False)
    result, d_out = lax.optimization_barrier((result, d_out))

    own, beside, far_off, diagonal, d_out = partials(side, d_out, down, True)
    result, own, beside, far_off, diagonal, d_out = lax.optimization_barrier(
        (result, own, beside, far_off, diagonal, d_out)
    )
    returned = exchange(result, everyone)
    diagonal = to_member(diagonal, 2)
    far_off = to_member(far_off, 2)
    beside = to_member((beside + diagonal.astype(F32)).astype(BF), 1)
    first, rest, own_weight = weight_parts(side, acts_flipped, d_out, slots // 8 * 3)
    d_act = own + far_off.astype(F32) + beside.astype(F32)
    d_hidden = (d_act * sigmoid * (1.0 + hidden * (1.0 - sigmoid))).astype(BF)
    d_hidden, first, rest, up = lax.optimization_barrier((d_hidden, first, rest, up))
    beside = to_member(d_hidden, 1)
    far_off = to_member(d_hidden, 2)
    up_held = hold(up)
    far_off, first = lax.optimization_barrier((far_off, first))
    d_hiddens = [d_hidden, beside, far_off, to_member(beside, 2)]
    first = to_mirror(first)
    (d_rows,) = merged(side, d_hiddens, up_held, True)
    d_rows, returned, first = lax.optimization_barrier((d_rows, returned, first))
    returned_dx = exchange(d_rows, everyone)
    rest = to_mirror(rest)

    layer_out, plain_held = combine(gated_flipped, [returned], plain_flipped)
    (grad_tokens,) = combine(plain_held, [returned_dx])
    grad_tokens, rest = lax.optimization_barrier((grad_tokens, rest))
    arrived = jnp.concatenate([first, rest])
    grad_weight = (own_weight.astype(F32) + arrived.astype(F32)).astype(BF)
    return (layer_out, grad_tokens, grad_weight[None])


def solution(mesh):
    in_specs = (
        P("expert", "pipe"),
        P("expert", "pipe"),
        P("expert", None),
        P("expert", None),
        P("expert", None),
        P("expert", None),
        P("expert", "pipe", None),
        P("expert", None, "pipe"),
    )
    out_specs = (P("expert", "pipe"), P("expert", "pipe"), P("expert", None, "pipe"))
    return jax.shard_map(shards, mesh=mesh, in_specs=in_specs, out_specs=out_specs, check_vma=False)
```

```python
import functools

import jax
import jax.numpy as jnp
from jax import lax
from jax.experimental import pallas as pl
from jax.experimental.pallas import tpu as pltpu
from jax.sharding import PartitionSpec as P

CAP = 16
BF = jnp.bfloat16
F32 = jnp.float32
RESIDENT = pl.BlockSpec(memory_space=pltpu.VMEM)
SCALARS = pl.BlockSpec(memory_space=pltpu.SMEM)
FAR = pl.BlockSpec(memory_space=pltpu.HBM)


def params():
    return pltpu.CompilerParams(vmem_limit_bytes=20 * 1024 * 1024)


def cost(flops, bytes_accessed):
    return pl.CostEstimate(flops=flops, bytes_accessed=bytes_accessed, transcendentals=0)


def near(array):
    return pltpu.with_memory_space_constraint(array, pltpu.VMEM)


def far(array):
    return pltpu.with_memory_space_constraint(array, pltpu.HBM)


def dot(a, b, ca, cb):
    return lax.dot_general(a, b, (((ca,), (cb,)), ((), ())), preferred_element_type=F32)


def column_block(width):
    for size in (256, 128):
        if width % size == 0:
            return size
    return width


def table_of(side_ref, ra_ref, rb_ref, ga_ref, gb_ref, expert_of, slots):
    upper = side_ref[1] == 1
    route = jnp.where(upper, rb_ref[...], ra_ref[...])
    gates = jnp.where(upper, gb_ref[...].astype(F32), ga_ref[...].astype(F32))
    top, tokens = route.shape
    experts = slots // CAP
    expert = lax.broadcasted_iota(jnp.int32, (experts, tokens), 0)
    member = jnp.zeros((experts, tokens), F32)
    gate = jnp.zeros((experts, tokens), F32)
    for k in range(top):
        named = route[k : k + 1, :] == expert
        member = member + jnp.where(named, 1.0, 0.0)
        gate = gate + jnp.where(named, gates[k : k + 1, :], 0.0)
    before = lax.broadcasted_iota(jnp.int32, (tokens, tokens), 0) < lax.broadcasted_iota(
        jnp.int32, (tokens, tokens), 1
    )
    earlier = dot(member.astype(BF), jnp.where(before, 1.0, 0.0).astype(BF), 1, 0)
    place = jnp.where(member > 0.5, earlier, 128.0).astype(BF)
    row = lax.broadcasted_iota(jnp.int32, (slots, experts), 0)
    column = lax.broadcasted_iota(jnp.int32, (slots, experts), 1)
    spread = jnp.where(expert_of(row // CAP) == column, 1.0, 0.0).astype(BF)
    place_rows = dot(spread, place, 1, 0)
    gate_rows = dot(spread, gate.astype(BF), 1, 0)
    slot = lax.broadcasted_iota(jnp.int32, (slots, tokens), 0) % CAP
    hit = place_rows == slot.astype(F32)
    return jnp.where(hit, 1.0, 0.0).astype(BF), jnp.where(hit, gate_rows, 0.0).astype(BF)


def fetch(source, target, sems, axis, parts):
    size = source.shape[axis] // parts
    copies = []
    for i in range(parts):
        span = tuple(pl.ds(i * size, size) if d == axis else slice(None) for d in range(2))
        copies.append(pltpu.make_async_copy(source.at[span], target.at[span], sems.at[i]))
    return copies


def streamed(source, target, sems, cols):
    step = pl.program_id(0)

    @pl.when(step == 0)
    def _():
        for copy in fetch(source, target, sems, 1, source.shape[1] // cols):
            copy.start()

    span = (slice(None), pl.ds(pl.multiple_of(step * cols, cols), cols))
    pltpu.make_async_copy(source.at[span], target.at[span], sems.at[step]).wait()
    return target[span]


def dispatch_kernel(side_ref, ra_ref, rb_ref, ga_ref, gb_ref, x_ref, *refs, depth, count):
    outs, flipped, (table_ref, x_all, out_all, sem, sems) = refs[:count], refs[count:-5], refs[-5:]
    routing = (side_ref, ra_ref, rb_ref, ga_ref, gb_ref)
    copy = pltpu.make_async_copy(x_ref, x_all, sem)

    def by_depth(block):
        return block // 2 % 2 * (2 * depth) + block // 4 * 2 + block % 2

    def by_plane(block):
        flip_x, flip_core = block // (2 * depth), block // depth % 2
        return (side_ref[2] ^ flip_x) * (2 * depth) + block % depth * 2 + (side_ref[3] ^ flip_core)

    copy.start()
    slots = table_ref.shape[0]
    if count == 1:
        table_ref[...] = table_of(*routing, by_depth, slots)[0]
    else:
        table_ref[...] = table_of(*routing, by_plane, slots)[1]
        for ref, table in zip(flipped, table_of(*routing, by_depth, slots)):
            ref[...] = table.T
    copy.wait()
    height, width = outs[0].shape
    cols = column_block(width)
    copies = []
    for k in range(width // cols):
        span = slice(k * cols, (k + 1) * cols)
        out_all[:, span] = dot(table_ref[...], x_all[:, span], 1, 0).astype(BF)
        for i, out_ref in enumerate(outs):
            source = out_all.at[i * height : (i + 1) * height, span]
            copies.append(pltpu.make_async_copy(source, out_ref.at[:, span], sems.at[len(copies)]))
            copies[-1].start()
    for copy in copies:
        copy.wait()


def dispatch(side, routing, x, slots, depth, count):
    tokens, width = x.shape
    tables = 0 if count == 1 else 2
    return pl.pallas_call(
        functools.partial(dispatch_kernel, depth=depth, count=count),
        in_specs=[SCALARS] + [RESIDENT] * 4 + [FAR],
        out_specs=[FAR] * count + [RESIDENT] * tables,
        out_shape=[pltpu.HBM((slots // count, width), BF)] * count
        + [jax.ShapeDtypeStruct((tokens, slots), BF)] * tables,
        scratch_shapes=[
            pltpu.VMEM((slots, tokens), BF),
            pltpu.VMEM((tokens, width), BF),
            pltpu.VMEM((slots, width), BF),
            pltpu.SemaphoreType.DMA,
            pltpu.SemaphoreType.DMA((count * (width // column_block(width)),)),
        ],
        compiler_params=params(),
        cost_estimate=cost(2 * slots * tokens * width, 2 * (slots + tokens) * width),
        name="dispatch",
    )(side, *[far(array) for array in routing], far(x))


def regroup_kernel(side_ref, *refs, members):
    pieces, (out_ref, held, sems) = refs[: len(members)], refs[-3:]
    arriving = [pltpu.make_async_copy(ref, held.at[i], sems.at[i]) for i, ref in enumerate(pieces)]
    leaving = []
    for copy in arriving:
        copy.start()
    for i, (j, copy) in enumerate(zip(members, arriving)):
        place = (side_ref[2] ^ (j // 2)) * 2 + (side_ref[3] ^ (j % 2))
        copy.wait()
        leaving.append(pltpu.make_async_copy(held.at[i], out_ref.at[:, place], sems.at[len(members) + i]))
        leaving[-1].start()
    for copy in leaving:
        copy.wait()


def regroup(side, pieces, depth, members, base=None):
    width = pieces[0].shape[1]
    pieces = [far(piece.reshape(depth, CAP, width)) for piece in pieces]
    more = [] if base is None else [far(base)]
    return pl.pallas_call(
        functools.partial(regroup_kernel, members=members),
        in_specs=[SCALARS] + [FAR] * (len(pieces) + len(more)),
        out_specs=FAR,
        out_shape=pltpu.HBM((depth, 4, CAP, width), BF),
        scratch_shapes=[
            pltpu.VMEM((len(members), depth, CAP, width), BF),
            pltpu.SemaphoreType.DMA((2 * len(members),)),
        ],
        input_output_aliases={1 + len(pieces): 0} if more else {},
        compiler_params=params(),
        cost_estimate=cost(0, 4 * CAP * depth * width * len(members)),
        name="regroup",
    )(side, *pieces, *more)


def hold_kernel(source, target, sems):
    copies = fetch(source, target, sems, 0, 4)
    for copy in copies:
        copy.start()
    for copy in copies:
        copy.wait()


def hold(weight):
    return pl.pallas_call(
        hold_kernel,
        in_specs=[FAR],
        out_specs=RESIDENT,
        out_shape=pltpu.VMEM(weight.shape, BF),
        scratch_shapes=[pltpu.SemaphoreType.DMA((4,))],
        compiler_params=params(),
        cost_estimate=cost(0, 4 * weight.size),
        name="hold",
    )(far(weight))


def partial_kernel(side_ref, x_ref, w_ref, own_ref, s1_ref, s2_ref, s3_ref, *refs, transposed):
    *kept, own_all, sent_all, sems = refs
    hid = own_ref.shape[1]
    copies = [pltpu.make_async_copy(x_ref, ref, sems.at[4]) for ref in kept]
    for copy in copies:
        copy.start()
    for j, ref in ((3, s3_ref), (1, s1_ref), (2, s2_ref), (0, own_ref)):
        block = pl.ds(pl.multiple_of((side_ref[0] ^ j) * hid, hid), hid)
        weight = w_ref[block, :] if transposed else w_ref[:, block]
        part = dot(x_ref[...], weight, 1, 1 if transposed else 0)
        held = sent_all.at[j - 1] if ref.dtype == BF else own_all.at[j]
        held[...] = part.astype(ref.dtype)
        copies.append(pltpu.make_async_copy(held, ref, sems.at[j]))
        copies[-1].start()
    for copy in copies:
        copy.wait()


def partials(side, x, w, transposed):
    rows, depth = x.shape
    hid = (w.shape[0] if transposed else w.shape[1]) // 4
    shapes = [pltpu.HBM((rows, hid), F32)] + [pltpu.HBM((rows, hid), BF)] * 3
    if transposed:
        shapes[1] = shapes[0]
        shapes.append(pltpu.HBM(x.shape, BF))
    return pl.pallas_call(
        functools.partial(partial_kernel, transposed=transposed),
        in_specs=[SCALARS, RESIDENT, RESIDENT],
        out_specs=[FAR] * len(shapes),
        out_shape=shapes,
        scratch_shapes=[
            pltpu.VMEM((2, rows, hid), F32),
            pltpu.VMEM((3, rows, hid), BF),
            pltpu.SemaphoreType.DMA((5,)),
        ],
        compiler_params=params(),
        cost_estimate=cost(8 * rows * depth * hid, 2 * (rows * depth + 4 * depth * hid) + 10 * rows * hid),
        name="partials",
    )(side, near(x), near(w))


def merge_kernel(side_ref, a0_ref, a1_ref, a2_ref, a3_ref, w_ref, out_ref, *refs, transposed):
    *flipped_ref, out_all, flipped, sems = refs
    pieces = (a0_ref, a1_ref, a2_ref, a3_ref)
    rows, hid = a0_ref.shape
    width = out_all.shape[1]
    cols = column_block(width)
    blocks = [pl.ds(pl.multiple_of((side_ref[0] ^ j) * hid, hid), hid) for j in range(4)]
    copies = []
    for i in range(width // cols):
        span = slice(i * cols, (i + 1) * cols)
        total = None
        for ref, block in zip(pieces, blocks):
            if transposed:
                part = dot(ref[...], w_ref[span, block], 1, 1)
            else:
                part = dot(ref[...], w_ref[block, span], 1, 0)
            total = part if total is None else total + part
        out_all[:, span] = total.astype(BF)
        copies.append(pltpu.make_async_copy(out_all.at[:, span], out_ref.at[:, span], sems.at[i]))
        copies[-1].start()
    if flipped_ref:
        for ref, block in zip(pieces, blocks):
            flipped[block, :] = ref[...].T
        copies.append(pltpu.make_async_copy(flipped, flipped_ref[0], sems.at[width // cols]))
        copies[-1].start()
    for copy in copies:
        copy.wait()


def merged(side, pieces, w, transposed):
    rows, hid = pieces[0].shape
    width = w.shape[0] if transposed else w.shape[1]
    shapes = [pltpu.HBM((rows, width), BF)]
    if not transposed:
        shapes.append(pltpu.HBM((4 * hid, rows), BF))
    return pl.pallas_call(
        functools.partial(merge_kernel, transposed=transposed),
        in_specs=[SCALARS] + [RESIDENT] * 5,
        out_specs=[FAR] * len(shapes),
        out_shape=shapes,
        scratch_shapes=[
            pltpu.VMEM((rows, width), BF),
            pltpu.VMEM((4 * hid, rows), BF),
            pltpu.SemaphoreType.DMA((width // column_block(width) + 1,)),
        ],
        compiler_params=params(),
        cost_estimate=cost(8 * rows * width * hid, 2 * (rows * width + 4 * width * hid + 4 * rows * hid)),
        name="merged",
    )(side, *pieces, near(w))


def weight_kernel(side_ref, act_ref, d_ref, own_ref, *refs):
    *sent_refs, d_all, sems = refs
    rows, cols = own_ref.shape
    d_out = streamed(d_ref, d_all, sems, cols)
    own = act_ref[pl.ds(pl.multiple_of(side_ref[1] * rows, rows), rows), :]
    other = act_ref[pl.ds(pl.multiple_of((1 - side_ref[1]) * rows, rows), rows), :]
    sent = dot(other, d_out, 1, 0).astype(BF)
    start = 0
    for ref in sent_refs:
        ref[...] = sent[start : start + ref.shape[0]]
        start += ref.shape[0]
    own_ref[...] = dot(own, d_out, 1, 0).astype(BF)


def weight_parts(side, acts, d_out, eighths):
    hid, rows = acts.shape
    width = d_out.shape[1]
    cols = column_block(width)
    heights = [hid // 2] + [hid // 16 * part for part in eighths]
    return pl.pallas_call(
        weight_kernel,
        grid=(width // cols,),
        in_specs=[SCALARS, pl.BlockSpec((hid, rows), lambda i: (0, 0)), FAR],
        out_specs=[pl.BlockSpec((height, cols), lambda i: (0, i)) for height in heights],
        out_shape=[pltpu.HBM((height, width), BF) for height in heights],
        scratch_shapes=[pltpu.VMEM((rows, width), BF), pltpu.SemaphoreType.DMA((width // cols,))],
        compiler_params=params(),
        cost_estimate=cost(2 * rows * width * hid, 2 * (rows * width + width * hid + rows * hid)),
        name="weight_parts",
    )(side, far(acts), far(d_out))


def add_kernel(part_ref, own_ref, out_ref, own, sems, *, start, step):
    rows = part_ref.shape[0]
    spans = [slice(i, i + step) for i in range(0, rows, step)]
    targets = [out_ref.at[start + span.start : start + span.stop, :] for span in spans]
    arriving = [
        pltpu.make_async_copy(target, own.at[span, :], sems.at[0, i])
        for i, (span, target) in enumerate(zip(spans, targets))
    ]
    for copy in arriving:
        copy.start()
    leaving = []
    for i, (span, target) in enumerate(zip(spans, targets)):
        arriving[i].wait()
        own[span, :] = (own[span, :].astype(F32) + part_ref[span, :].astype(F32)).astype(BF)
        leaving.append(pltpu.make_async_copy(own.at[span, :], target, sems.at[1, i]))
        leaving[i].start()
    for copy in leaving:
        copy.wait()


def add_rows(own, part, start):
    rows, width = part.shape
    step = 64
    return pl.pallas_call(
        functools.partial(add_kernel, start=start, step=step),
        in_specs=[RESIDENT, FAR],
        out_specs=FAR,
        out_shape=pltpu.HBM(own.shape, BF),
        scratch_shapes=[pltpu.VMEM((rows, width), BF), pltpu.SemaphoreType.DMA((2, rows // step))],
        input_output_aliases={1: 0},
        compiler_params=params(),
        cost_estimate=cost(rows * width, 6 * rows * width),
        name="add_rows",
    )(part, far(own))


def combine_kernel(*refs, count, kept):
    table_ref, parts, refs = refs[0], refs[1 : count + 1], refs[count + 1 :]
    if kept:
        next_ref, out_ref, next_out, out_all, sems = refs
    else:
        out_ref, out_all, sems = refs
    copies = []
    tokens, width = out_all.shape
    cols, rows = column_block(width), parts[0].shape[0]
    for i in range(width // cols):
        span = (slice(None), slice(i * cols, (i + 1) * cols))
        total = None
        for k, ref in enumerate(parts):
            part = dot(table_ref[:, k * rows : (k + 1) * rows], ref[span], 1, 0)
            total = part if total is None else total + part
        out_all[span] = total.astype(BF)
        copies.append(pltpu.make_async_copy(out_all.at[span], out_ref.at[span], sems.at[i]))
        copies[-1].start()
    if kept:
        next_out[...] = next_ref[...]
    for copy in copies:
        copy.wait()


def combine(table, parts, following=None):
    tokens, slots = table.shape
    width = parts[0].shape[1]
    kept = following is not None
    return pl.pallas_call(
        functools.partial(combine_kernel, count=len(parts), kept=kept),
        in_specs=[RESIDENT] * (1 + len(parts) + kept),
        out_specs=[FAR] + [RESIDENT] * kept,
        out_shape=[pltpu.HBM((tokens, width), BF)] + [pltpu.VMEM(table.shape, BF)] * kept,
        scratch_shapes=[pltpu.VMEM((tokens, width), BF), pltpu.SemaphoreType.DMA((width // column_block(width),))],
        compiler_params=params(),
        cost_estimate=cost(2 * slots * tokens * width, 2 * (slots + tokens) * width),
        name="combine",
    )(*((table, *parts, following) if kept else (near(table), *[near(part) for part in parts])))


def to_member(block, flip):
    count = lax.axis_size("pipe")
    return lax.ppermute(block, "pipe", [(p, p ^ flip) for p in range(count)])


def to_members(blocks):
    return [to_member(block, j + 1) for j, block in enumerate(blocks)]


def to_mirror(block):
    count = lax.axis_size("pipe")
    return lax.ppermute(block, "pipe", [(p, count - 1 - p) for p in range(count)])


def exchange(rows, groups):
    ranks = len(groups[0])
    blocks = rows.reshape(ranks, rows.shape[0] // ranks, -1)
    blocks = lax.all_to_all(
        blocks, "expert", split_axis=0, concat_axis=0, tiled=True, axis_index_groups=groups
    )
    return blocks.reshape(rows.shape)


def shards(tokens, cotangent, route_a, route_b, gates_a, gates_b, w_up, w_down):
    half_size = lax.axis_size("pipe") // 2
    experts = lax.axis_size("expert")
    slots, depth = experts * CAP, experts // 4
    up, down = w_up[0], w_down[0]
    pipe, expert = lax.axis_index("pipe"), lax.axis_index("expert")
    side = [pipe % half_size, pipe // half_size, expert // (2 * depth), expert % 2]
    side = jnp.stack(side).astype(jnp.int32)
    columns = [[(x * depth + z) * 2 + core for z in range(depth)] for x in range(2) for core in range(2)]
    everyone = [[column[z] for z in range(depth) for column in columns]]

    routing = [route_a.T, route_b.T, gates_a.T, gates_b.T]
    (sent_x,) = dispatch(side, routing, tokens, slots, depth, 1)
    rows_x = exchange(sent_x, everyone)
    *pieces, plain_flipped, gated_flipped = dispatch(side, routing, cotangent, slots, depth, 4)
    for j in range(1, 4):
        flip = j // 2 * (2 * depth) + j % 2
        pieces[j] = lax.ppermute(pieces[j], "expert", [(e, e ^ flip) for e in range(experts)])
    grouped = regroup(side, pieces[:3], depth, (0, 1, 2))
    grouped, rows_x, pieces[3] = lax.optimization_barrier((grouped, rows_x, pieces[3]))
    grouped = regroup(side, pieces[3:], depth, (3,), grouped).reshape(slots, -1)
    d_out = exchange(grouped, columns)
    own, *others = partials(side, rows_x, up, False)
    hidden = own + sum(block.astype(F32) for block in to_members(others))
    sigmoid = jax.nn.sigmoid(hidden)
    act = (hidden * sigmoid).astype(BF)
    act, down = lax.optimization_barrier((act, down))
    down_held = hold(down)
    acts = [act] + to_members([act] * 3)
    result, acts_flipped = merged(side, acts, down_held, False)
    result, d_out = lax.optimization_barrier((result, d_out))

    returned = exchange(result, everyone)
    own, beside, far_off, diagonal, d_out = partials(side, d_out, down, True)
    diagonal = to_member(diagonal, 2)
    far_off = to_member(far_off, 2)
    beside = to_member((beside + diagonal.astype(F32)).astype(BF), 1)
    own_weight, first, rest, last = weight_parts(side, acts_flipped, d_out, (3, 3, 2))
    d_act = own + far_off.astype(F32) + beside.astype(F32)
    d_hidden = (d_act * sigmoid * (1.0 + hidden * (1.0 - sigmoid))).astype(BF)
    d_hidden, first, rest, last, up = lax.optimization_barrier((d_hidden, first, rest, last, up))
    beside = to_member(d_hidden, 1)
    far_off = to_member(d_hidden, 2)
    up_held = hold(up)
    far_off, first = lax.optimization_barrier((far_off, first))
    d_hiddens = [d_hidden, beside, far_off, to_member(beside, 2)]
    first = to_mirror(first)
    (d_rows,) = merged(side, d_hiddens, up_held, True)
    d_rows, returned, first = lax.optimization_barrier((d_rows, returned, first))
    returned_dx = exchange(d_rows, everyone)
    rest, last = to_mirror(rest), to_mirror(last)

    layer_out, plain_held = combine(gated_flipped, [returned], plain_flipped)
    height = first.shape[0]
    grad_weight = add_rows(add_rows(own_weight, first, 0), rest, height)
    (grad_tokens,) = combine(plain_held, [returned_dx])
    grad_tokens, last, grad_weight = lax.optimization_barrier((grad_tokens, last, grad_weight))
    grad_weight = add_rows(grad_weight, last, height + rest.shape[0])
    return (layer_out, grad_tokens, grad_weight[None])


def solution(mesh):
    in_specs = (
        P("expert", "pipe"),
        P("expert", "pipe"),
        P("expert", None),
        P("expert", None),
        P("expert", None),
        P("expert", None),
        P("expert", "pipe", None),
        P("expert", None, "pipe"),
    )
    out_specs = (P("expert", "pipe"), P("expert", "pipe"), P("expert", None, "pipe"))
    return jax.shard_map(shards, mesh=mesh, in_specs=in_specs, out_specs=out_specs, check_vma=False)
```

```python
import functools

import jax
import jax.numpy as jnp
from jax import lax
from jax.experimental import pallas as pl
from jax.experimental.pallas import tpu as pltpu
from jax.sharding import PartitionSpec as P

CAP = 16
BF = jnp.bfloat16
F32 = jnp.float32
RESIDENT = pl.BlockSpec(memory_space=pltpu.VMEM)
SCALARS = pl.BlockSpec(memory_space=pltpu.SMEM)
FAR = pl.BlockSpec(memory_space=pltpu.HBM)


def params():
    return pltpu.CompilerParams(vmem_limit_bytes=20 * 1024 * 1024)


def cost(flops, bytes_accessed):
    return pl.CostEstimate(flops=flops, bytes_accessed=bytes_accessed, transcendentals=0)


def near(array):
    return pltpu.with_memory_space_constraint(array, pltpu.VMEM)


def far(array):
    return pltpu.with_memory_space_constraint(array, pltpu.HBM)


def dot(a, b, ca, cb):
    return lax.dot_general(a, b, (((ca,), (cb,)), ((), ())), preferred_element_type=F32)


def column_block(width):
    for size in (256, 128):
        if width % size == 0:
            return size
    return width


def table_of(side_ref, ra_ref, rb_ref, ga_ref, gb_ref, expert_of, slots):
    upper = side_ref[1] == 1
    route = jnp.where(upper, rb_ref[...], ra_ref[...])
    gates = jnp.where(upper, gb_ref[...].astype(F32), ga_ref[...].astype(F32))
    top, tokens = route.shape
    experts = slots // CAP
    expert = lax.broadcasted_iota(jnp.int32, (experts, tokens), 0)
    member = jnp.zeros((experts, tokens), F32)
    gate = jnp.zeros((experts, tokens), F32)
    for k in range(top):
        named = route[k : k + 1, :] == expert
        member = member + jnp.where(named, 1.0, 0.0)
        gate = gate + jnp.where(named, gates[k : k + 1, :], 0.0)
    before = lax.broadcasted_iota(jnp.int32, (tokens, tokens), 0) < lax.broadcasted_iota(
        jnp.int32, (tokens, tokens), 1
    )
    earlier = dot(member.astype(BF), jnp.where(before, 1.0, 0.0).astype(BF), 1, 0)
    place = jnp.where(member > 0.5, earlier, 128.0).astype(BF)
    row = lax.broadcasted_iota(jnp.int32, (slots, experts), 0)
    column = lax.broadcasted_iota(jnp.int32, (slots, experts), 1)
    spread = jnp.where(expert_of(row // CAP) == column, 1.0, 0.0).astype(BF)
    place_rows = dot(spread, place, 1, 0)
    gate_rows = dot(spread, gate.astype(BF), 1, 0)
    slot = lax.broadcasted_iota(jnp.int32, (slots, tokens), 0) % CAP
    hit = place_rows == slot.astype(F32)
    return jnp.where(hit, 1.0, 0.0).astype(BF), jnp.where(hit, gate_rows, 0.0).astype(BF)


def fetch(source, target, sems, axis, parts):
    size = source.shape[axis] // parts
    copies = []
    for i in range(parts):
        span = tuple(pl.ds(i * size, size) if d == axis else slice(None) for d in range(2))
        copies.append(pltpu.make_async_copy(source.at[span], target.at[span], sems.at[i]))
    return copies


def streamed(source, target, sems, cols):
    step = pl.program_id(0)

    @pl.when(step == 0)
    def _():
        for copy in fetch(source, target, sems, 1, source.shape[1] // cols):
            copy.start()

    span = (slice(None), pl.ds(pl.multiple_of(step * cols, cols), cols))
    pltpu.make_async_copy(source.at[span], target.at[span], sems.at[step]).wait()
    return target[span]


def dispatch_kernel(side_ref, ra_ref, rb_ref, ga_ref, gb_ref, x_ref, *refs, depth, count):
    outs, flipped, (table_ref, x_all, out_all, sem, sems) = refs[:count], refs[count:-5], refs[-5:]
    routing = (side_ref, ra_ref, rb_ref, ga_ref, gb_ref)
    copy = pltpu.make_async_copy(x_ref, x_all, sem)

    def by_depth(block):
        return block // 2 % 2 * (2 * depth) + block // 4 * 2 + block % 2

    def by_plane(block):
        flip_x, flip_core = block // (2 * depth), block // depth % 2
        return (side_ref[2] ^ flip_x) * (2 * depth) + block % depth * 2 + (side_ref[3] ^ flip_core)

    copy.start()
    slots = table_ref.shape[0]
    if count == 1:
        table_ref[...] = table_of(*routing, by_depth, slots)[0]
    else:
        table_ref[...] = table_of(*routing, by_plane, slots)[1]
        for ref, table in zip(flipped, table_of(*routing, by_depth, slots)):
            ref[...] = table.T
    copy.wait()
    height, width = outs[0].shape
    cols = column_block(width)
    copies = []
    for k in range(width // cols):
        span = slice(k * cols, (k + 1) * cols)
        out_all[:, span] = dot(table_ref[...], x_all[:, span], 1, 0).astype(BF)
        for i, out_ref in enumerate(outs):
            source = out_all.at[i * height : (i + 1) * height, span]
            copies.append(pltpu.make_async_copy(source, out_ref.at[:, span], sems.at[len(copies)]))
            copies[-1].start()
    for copy in copies:
        copy.wait()


def dispatch(side, routing, x, slots, depth, count):
    tokens, width = x.shape
    tables = 0 if count == 1 else 2
    return pl.pallas_call(
        functools.partial(dispatch_kernel, depth=depth, count=count),
        in_specs=[SCALARS] + [RESIDENT] * 4 + [FAR],
        out_specs=[FAR] * count + [RESIDENT] * tables,
        out_shape=[pltpu.HBM((slots // count, width), BF)] * count
        + [jax.ShapeDtypeStruct((tokens, slots), BF)] * tables,
        scratch_shapes=[
            pltpu.VMEM((slots, tokens), BF),
            pltpu.VMEM((tokens, width), BF),
            pltpu.VMEM((slots, width), BF),
            pltpu.SemaphoreType.DMA,
            pltpu.SemaphoreType.DMA((count * (width // column_block(width)),)),
        ],
        compiler_params=params(),
        cost_estimate=cost(2 * slots * tokens * width, 2 * (slots + tokens) * width),
        name="dispatch",
    )(side, *[far(array) for array in routing], far(x))


def regroup_kernel(side_ref, *refs, members):
    pieces, (out_ref, held, sems) = refs[: len(members)], refs[-3:]
    depth = held.shape[1]
    cuts = [slice(z, z + depth // 4) for z in range(0, depth, depth // 4)]
    arriving, leaving = [], []
    for i, ref in enumerate(pieces):
        for cut in cuts:
            copy = pltpu.make_async_copy(ref.at[cut], held.at[i, cut], sems.at[0, len(arriving)])
            copy.start()
            arriving.append((i, cut, copy))
    for i, cut, copy in arriving:
        place = (side_ref[2] ^ (members[i] // 2)) * 2 + (side_ref[3] ^ (members[i] % 2))
        copy.wait()
        leaving.append(
            pltpu.make_async_copy(held.at[i, cut], out_ref.at[cut, place], sems.at[1, len(leaving)])
        )
        leaving[-1].start()
    for copy in leaving:
        copy.wait()


def regroup(side, pieces, depth, members, base=None):
    width = pieces[0].shape[1]
    pieces = [far(piece.reshape(depth, CAP, width)) for piece in pieces]
    more = [] if base is None else [far(base)]
    return pl.pallas_call(
        functools.partial(regroup_kernel, members=members),
        in_specs=[SCALARS] + [FAR] * (len(pieces) + len(more)),
        out_specs=FAR,
        out_shape=pltpu.HBM((depth, 4, CAP, width), BF),
        scratch_shapes=[
            pltpu.VMEM((len(members), depth, CAP, width), BF),
            pltpu.SemaphoreType.DMA((2, 4 * len(members))),
        ],
        input_output_aliases={1 + len(pieces): 0} if more else {},
        compiler_params=params(),
        cost_estimate=cost(0, 4 * CAP * depth * width * len(members)),
        name="regroup",
    )(side, *pieces, *more)


def hold_kernel(source, target, sems):
    copies = fetch(source, target, sems, 0, 4)
    for copy in copies:
        copy.start()
    for copy in copies:
        copy.wait()


def hold(weight):
    return pl.pallas_call(
        hold_kernel,
        in_specs=[FAR],
        out_specs=RESIDENT,
        out_shape=pltpu.VMEM(weight.shape, BF),
        scratch_shapes=[pltpu.SemaphoreType.DMA((4,))],
        compiler_params=params(),
        cost_estimate=cost(0, 4 * weight.size),
        name="hold",
    )(far(weight))


def partial_kernel(side_ref, x_ref, w_ref, own_ref, s1_ref, s2_ref, s3_ref, *refs, transposed):
    *kept, own_all, sent_all, sems = refs
    hid = own_ref.shape[1]
    copies = [pltpu.make_async_copy(x_ref, ref, sems.at[4]) for ref in kept]
    for copy in copies:
        copy.start()
    for j, ref in ((3, s3_ref), (1, s1_ref), (2, s2_ref), (0, own_ref)):
        block = pl.ds(pl.multiple_of((side_ref[0] ^ j) * hid, hid), hid)
        weight = w_ref[block, :] if transposed else w_ref[:, block]
        part = dot(x_ref[...], weight, 1, 1 if transposed else 0)
        held = sent_all.at[j - 1] if ref.dtype == BF else own_all.at[j]
        held[...] = part.astype(ref.dtype)
        copies.append(pltpu.make_async_copy(held, ref, sems.at[j]))
        copies[-1].start()
    for copy in copies:
        copy.wait()


def partials(side, x, w, transposed):
    rows, depth = x.shape
    hid = (w.shape[0] if transposed else w.shape[1]) // 4
    shapes = [pltpu.HBM((rows, hid), F32)] + [pltpu.HBM((rows, hid), BF)] * 3
    if transposed:
        shapes[1] = shapes[0]
        shapes.append(pltpu.HBM(x.shape, BF))
    return pl.pallas_call(
        functools.partial(partial_kernel, transposed=transposed),
        in_specs=[SCALARS, RESIDENT, RESIDENT],
        out_specs=[FAR] * len(shapes),
        out_shape=shapes,
        scratch_shapes=[
            pltpu.VMEM((2, rows, hid), F32),
            pltpu.VMEM((3, rows, hid), BF),
            pltpu.SemaphoreType.DMA((5,)),
        ],
        compiler_params=params(),
        cost_estimate=cost(8 * rows * depth * hid, 2 * (rows * depth + 4 * depth * hid) + 10 * rows * hid),
        name="partials",
    )(side, near(x), near(w))


def merge_kernel(side_ref, a0_ref, a1_ref, a2_ref, a3_ref, w_ref, out_ref, *refs, transposed):
    *flipped_ref, out_all, flipped, sems = refs
    pieces = (a0_ref, a1_ref, a2_ref, a3_ref)
    rows, hid = a0_ref.shape
    width = out_all.shape[1]
    cols = column_block(width)
    blocks = [pl.ds(pl.multiple_of((side_ref[0] ^ j) * hid, hid), hid) for j in range(4)]
    copies = []
    for i in range(width // cols):
        span = slice(i * cols, (i + 1) * cols)
        total = None
        for ref, block in zip(pieces, blocks):
            if transposed:
                part = dot(ref[...], w_ref[span, block], 1, 1)
            else:
                part = dot(ref[...], w_ref[block, span], 1, 0)
            total = part if total is None else total + part
        out_all[:, span] = total.astype(BF)
        copies.append(pltpu.make_async_copy(out_all.at[:, span], out_ref.at[:, span], sems.at[i]))
        copies[-1].start()
    if flipped_ref:
        for ref, block in zip(pieces, blocks):
            flipped[block, :] = ref[...].T
        copies.append(pltpu.make_async_copy(flipped, flipped_ref[0], sems.at[width // cols]))
        copies[-1].start()
    for copy in copies:
        copy.wait()


def merged(side, pieces, w, transposed):
    rows, hid = pieces[0].shape
    width = w.shape[0] if transposed else w.shape[1]
    shapes = [pltpu.HBM((rows, width), BF)]
    if not transposed:
        shapes.append(pltpu.HBM((4 * hid, rows), BF))
    return pl.pallas_call(
        functools.partial(merge_kernel, transposed=transposed),
        in_specs=[SCALARS] + [RESIDENT] * 5,
        out_specs=[FAR] * len(shapes),
        out_shape=shapes,
        scratch_shapes=[
            pltpu.VMEM((rows, width), BF),
            pltpu.VMEM((4 * hid, rows), BF),
            pltpu.SemaphoreType.DMA((width // column_block(width) + 1,)),
        ],
        compiler_params=params(),
        cost_estimate=cost(8 * rows * width * hid, 2 * (rows * width + 4 * width * hid + 4 * rows * hid)),
        name="merged",
    )(side, *pieces, near(w))


def weight_kernel(side_ref, act_ref, d_ref, own_ref, *refs):
    *sent_refs, d_all, sems = refs
    rows, cols = own_ref.shape
    d_out = streamed(d_ref, d_all, sems, cols)
    own = act_ref[pl.ds(pl.multiple_of(side_ref[1] * rows, rows), rows), :]
    other = act_ref[pl.ds(pl.multiple_of((1 - side_ref[1]) * rows, rows), rows), :]
    sent = dot(other, d_out, 1, 0).astype(BF)
    start = 0
    for ref in sent_refs:
        ref[...] = sent[start : start + ref.shape[0]]
        start += ref.shape[0]
    own_ref[...] = dot(own, d_out, 1, 0).astype(BF)


def weight_parts(side, acts, d_out, eighths):
    hid, rows = acts.shape
    width = d_out.shape[1]
    cols = column_block(width)
    heights = [hid // 2] + [hid // 16 * part for part in eighths]
    return pl.pallas_call(
        weight_kernel,
        grid=(width // cols,),
        in_specs=[SCALARS, pl.BlockSpec((hid, rows), lambda i: (0, 0)), FAR],
        out_specs=[pl.BlockSpec((height, cols), lambda i: (0, i)) for height in heights],
        out_shape=[pltpu.HBM((height, width), BF) for height in heights],
        scratch_shapes=[pltpu.VMEM((rows, width), BF), pltpu.SemaphoreType.DMA((width // cols,))],
        compiler_params=params(),
        cost_estimate=cost(2 * rows * width * hid, 2 * (rows * width + width * hid + rows * hid)),
        name="weight_parts",
    )(side, far(acts), far(d_out))


def add_kernel(part_ref, own_ref, out_ref, own, sems, *, start, step):
    rows = part_ref.shape[0]
    spans = [slice(i, i + step) for i in range(0, rows, step)]
    targets = [out_ref.at[start + span.start : start + span.stop, :] for span in spans]
    arriving = [
        pltpu.make_async_copy(target, own.at[span, :], sems.at[0, i])
        for i, (span, target) in enumerate(zip(spans, targets))
    ]
    for copy in arriving:
        copy.start()
    leaving = []
    for i, (span, target) in enumerate(zip(spans, targets)):
        arriving[i].wait()
        own[span, :] = (own[span, :].astype(F32) + part_ref[span, :].astype(F32)).astype(BF)
        leaving.append(pltpu.make_async_copy(own.at[span, :], target, sems.at[1, i]))
        leaving[i].start()
    for copy in leaving:
        copy.wait()


def add_rows(own, part, start):
    rows, width = part.shape
    step = 32
    return pl.pallas_call(
        functools.partial(add_kernel, start=start, step=step),
        in_specs=[RESIDENT, FAR],
        out_specs=FAR,
        out_shape=pltpu.HBM(own.shape, BF),
        scratch_shapes=[pltpu.VMEM((rows, width), BF), pltpu.SemaphoreType.DMA((2, rows // step))],
        input_output_aliases={1: 0},
        compiler_params=params(),
        cost_estimate=cost(rows * width, 6 * rows * width),
        name="add_rows",
    )(part, far(own))


def combine_kernel(*refs, count, kept):
    table_ref, parts, refs = refs[0], refs[1 : count + 1], refs[count + 1 :]
    if kept:
        next_ref, out_ref, next_out, out_all, sems = refs
    else:
        out_ref, out_all, sems = refs
    copies = []
    tokens, width = out_all.shape
    cols, rows = column_block(width), parts[0].shape[0]
    for i in range(width // cols):
        span = (slice(None), slice(i * cols, (i + 1) * cols))
        total = None
        for k, ref in enumerate(parts):
            part = dot(table_ref[:, k * rows : (k + 1) * rows], ref[span], 1, 0)
            total = part if total is None else total + part
        out_all[span] = total.astype(BF)
        copies.append(pltpu.make_async_copy(out_all.at[span], out_ref.at[span], sems.at[i]))
        copies[-1].start()
    if kept:
        next_out[...] = next_ref[...]
    for copy in copies:
        copy.wait()


def combine(table, parts, following=None):
    tokens, slots = table.shape
    width = parts[0].shape[1]
    kept = following is not None
    return pl.pallas_call(
        functools.partial(combine_kernel, count=len(parts), kept=kept),
        in_specs=[RESIDENT] * (1 + len(parts) + kept),
        out_specs=[FAR] + [RESIDENT] * kept,
        out_shape=[pltpu.HBM((tokens, width), BF)] + [pltpu.VMEM(table.shape, BF)] * kept,
        scratch_shapes=[pltpu.VMEM((tokens, width), BF), pltpu.SemaphoreType.DMA((width // column_block(width),))],
        compiler_params=params(),
        cost_estimate=cost(2 * slots * tokens * width, 2 * (slots + tokens) * width),
        name="combine",
    )(*((table, *parts, following) if kept else (near(table), *[near(part) for part in parts])))


def to_member(block, flip):
    count = lax.axis_size("pipe")
    return lax.ppermute(block, "pipe", [(p, p ^ flip) for p in range(count)])


def to_members(blocks):
    return [to_member(block, j + 1) for j, block in enumerate(blocks)]


def to_mirror(block):
    count = lax.axis_size("pipe")
    return lax.ppermute(block, "pipe", [(p, count - 1 - p) for p in range(count)])


def exchange(rows, groups):
    ranks = len(groups[0])
    blocks = rows.reshape(ranks, rows.shape[0] // ranks, -1)
    blocks = lax.all_to_all(
        blocks, "expert", split_axis=0, concat_axis=0, tiled=True, axis_index_groups=groups
    )
    return blocks.reshape(rows.shape)


def shards(tokens, cotangent, route_a, route_b, gates_a, gates_b, w_up, w_down):
    half_size = lax.axis_size("pipe") // 2
    experts = lax.axis_size("expert")
    slots, depth = experts * CAP, experts // 4
    up, down = w_up[0], w_down[0]
    pipe, expert = lax.axis_index("pipe"), lax.axis_index("expert")
    side = [pipe % half_size, pipe // half_size, expert // (2 * depth), expert % 2]
    side = jnp.stack(side).astype(jnp.int32)
    columns = [[(x * depth + z) * 2 + core for z in range(depth)] for x in range(2) for core in range(2)]
    everyone = [[column[z] for z in range(depth) for column in columns]]

    routing = [route_a.T, route_b.T, gates_a.T, gates_b.T]
    (sent_x,) = dispatch(side, routing, tokens, slots, depth, 1)
    rows_x = exchange(sent_x, everyone)
    *pieces, plain_flipped, gated_flipped = dispatch(side, routing, cotangent, slots, depth, 4)
    for j in range(1, 4):
        flip = j // 2 * (2 * depth) + j % 2
        pieces[j] = lax.ppermute(pieces[j], "expert", [(e, e ^ flip) for e in range(experts)])
    grouped = regroup(side, pieces[:3], depth, (0, 1, 2))
    grouped, rows_x, pieces[3] = lax.optimization_barrier((grouped, rows_x, pieces[3]))
    grouped = regroup(side, pieces[3:], depth, (3,), grouped).reshape(slots, -1)
    d_out = exchange(grouped, columns)
    own, *others = partials(side, rows_x, up, False)
    hidden = own + sum(block.astype(F32) for block in to_members(others))
    sigmoid = jax.nn.sigmoid(hidden)
    act = (hidden * sigmoid).astype(BF)
    act, down = lax.optimization_barrier((act, down))
    down_held = hold(down)
    acts = [act] + to_members([act] * 3)
    result, acts_flipped = merged(side, acts, down_held, False)
    result, d_out = lax.optimization_barrier((result, d_out))

    returned = exchange(result, everyone)
    own, beside, far_off, diagonal, d_out = partials(side, d_out, down, True)
    diagonal = to_member(diagonal, 2)
    far_off = to_member(far_off, 2)
    beside = to_member((beside + diagonal.astype(F32)).astype(BF), 1)
    own_weight, first, rest, last = weight_parts(side, acts_flipped, d_out, (3, 3, 2))
    d_act = own + far_off.astype(F32) + beside.astype(F32)
    d_hidden = (d_act * sigmoid * (1.0 + hidden * (1.0 - sigmoid))).astype(BF)
    d_hidden, first, rest, last, up = lax.optimization_barrier((d_hidden, first, rest, last, up))
    beside = to_member(d_hidden, 1)
    far_off = to_member(d_hidden, 2)
    up_held = hold(up)
    far_off, first = lax.optimization_barrier((far_off, first))
    d_hiddens = [d_hidden, beside, far_off, to_member(beside, 2)]
    first = to_mirror(first)
    (d_rows,) = merged(side, d_hiddens, up_held, True)
    d_rows, returned, first = lax.optimization_barrier((d_rows, returned, first))
    returned_dx = exchange(d_rows, everyone)
    rest, last = to_mirror(rest), to_mirror(last)

    layer_out, plain_held = combine(gated_flipped, [returned], plain_flipped)
    height = first.shape[0]
    grad_weight = add_rows(add_rows(own_weight, first, 0), rest, height)
    (grad_tokens,) = combine(plain_held, [returned_dx])
    grad_tokens, last, grad_weight = lax.optimization_barrier((grad_tokens, last, grad_weight))
    grad_weight = add_rows(grad_weight, last, height + rest.shape[0])
    return (layer_out, grad_tokens, grad_weight[None])


def solution(mesh):
    in_specs = (
        P("expert", "pipe"),
        P("expert", "pipe"),
        P("expert", None),
        P("expert", None),
        P("expert", None),
        P("expert", None),
        P("expert", "pipe", None),
        P("expert", None, "pipe"),
    )
    out_specs = (P("expert", "pipe"), P("expert", "pipe"), P("expert", None, "pipe"))
    return jax.shard_map(shards, mesh=mesh, in_specs=in_specs, out_specs=out_specs, check_vma=False)
```
